256 devices in a mesh: lat: 64 (over x_lo, z, y), lon: 4 (over x_hi, core).
Axes of the slice: x: 4 (x_hi: 2, x_lo: 2; x = x_hi * 2 + x_lo), y: 4, z: 8, core: 2. Of those that a mesh axis runs over, the one named last changes fastest.
Arguments:
- grid_field: bfloat16 [512, 1024, 256], P('lat', 'lon'), may hold values from -6 to 6
- basis_index: int32 [512, 25], P('lat'), may hold values from 0 to 4
- quad_weight: bfloat16 [512, 25], P('lat'), may hold values from 0.19921875 to 1
- disco_weight: bfloat16 [4, 2, 128, 128], replicated, may hold values from -0.25 to 0.25
- mode_order: int32 [512], replicated, may hold values from 0 to 511, each once
- legendre: bfloat16 [512, 512, 512], P(('lat', 'lon')), may hold values from -0.25 to 0.25
- filter_weight: bfloat16 [2, 256, 256], replicated, may hold values from -0.25 to 0.25
- inner_weight: bfloat16 [256, 512], replicated, may hold values from -0.375 to 0.375
- outer_weight: bfloat16 [512, 256], replicated, may hold values from -0.25 to 0.25
Outputs:
- layer_out: bfloat16 [512, 1024, 256], P('lat', 'lon')
The draws below stay inside these ranges and needn't reach their ends.
Inputs may be any that keep to these rules, and one draw needn't show every extreme that they name: `basis_index`: A value below 4 names the basis function of a support point; the value 4 marks a point outside the filter's support. `mode_order`: every wavenumber 0 to 511 is held by exactly one slot.
All inputs are finite; a program needn't handle non-finite values.
Results may differ from the reference program's by a relative error of at most 0.017.
Values may be sent and summed in bfloat16 or wider, within the bound.
A program may use at most 128 MiB of HBM per device.

```python
import math
import jax
import jax.numpy as jnp
from jax import lax

CHANNELS = 256
GROUPS = 2
GROUP_CH = 128
BASES = 4
HIDDEN_SIZE = 512
NLON = 1024
NLAT = 512
MODES = 512
DEGREES = 512


def with_ends(array, key, least, top_value):
    extent = array.shape
    place = [jax.random.randint(jax.random.fold_in(key, axis), (), 0, extent[axis]) for axis in range(len(extent))]
    array = array.at[tuple(place)].set(least)
    longest = extent.index(max(extent))
    place[longest] = (place[longest] + 1) % extent[longest]
    return array.at[tuple(place)].set(top_value)


def block_levels(stream_key, dims, split, low, high):
    def one(position, shards_of):
        draws = jax.random.uniform(jax.random.fold_in(jax.random.fold_in(stream_key, 6), position), (shards_of,), jnp.float32, low / len(split), high / len(split))
        return jnp.repeat(jnp.exp(draws), dims[position] // shards_of).reshape((-1,) + (1,) * (len(dims) - position - 1))

    factor_of = one(*split[0])
    for cut in split[1:]:
        factor_of = factor_of * one(*cut)
    return factor_of


def normal_values(rng, shape, width, most, pieces=(), kind=jnp.bfloat16):
    values = jax.random.normal(rng, shape, jnp.float32) * width
    if len(pieces) > 0:
        values = block_levels(rng, shape, pieces, -0.22, 0.18) * values
    return jnp.clip(values, min=-most, max=most).astype(kind)


def setup_inputs(seed: int = 0) -> dict:
    streams_of = jax.random.split(jax.random.key(seed), 10)
    grid_field = normal_values(streams_of[0], (NLAT, NLON, CHANNELS), 1.0, 6.0, ((0, 64), (1, 4)))
    basis_index = with_ends(jax.random.randint(streams_of[1], (NLAT, 25), 0, BASES + 1), jax.random.fold_in(streams_of[1], 1), 0, BASES).astype(jnp.int32)
    quad_weight = jnp.clip(0.19921875 + 0.80078125 * jax.random.uniform(streams_of[2], (NLAT, 25), jnp.float32) ** block_levels(streams_of[2], (NLAT, 25), ((0, 64),), -0.2, 0.2), 0.19921875, 1.0).astype(jnp.bfloat16)
    disco_weight = normal_values(streams_of[3], (BASES, GROUPS, GROUP_CH, GROUP_CH), (BASES * GROUP_CH) ** -0.5, 0.25)
    mode_order = jax.random.permutation(streams_of[4], MODES).astype(jnp.int32)
    legendre = normal_values(streams_of[5], (MODES, DEGREES, NLAT), NLAT ** -0.5, 0.25, ((0, 256),))
    filter_weight = normal_values(streams_of[6], (2, CHANNELS, CHANNELS), (2 * CHANNELS) ** -0.5, 0.25)
    inner_weight = normal_values(streams_of[7], (CHANNELS, HIDDEN_SIZE), CHANNELS ** -0.5, 0.375)
    outer_weight = normal_values(streams_of[8], (HIDDEN_SIZE, CHANNELS), HIDDEN_SIZE ** -0.5, 0.25)
    return {"grid_field": grid_field, "basis_index": basis_index, "quad_weight": quad_weight, "disco_weight": disco_weight, "mode_order": mode_order, "legendre": legendre, "filter_weight": filter_weight, "inner_weight": inner_weight, "outer_weight": outer_weight}


def twiddle(mode_ids, places, full_len, doubled):
    residue = (mode_ids[:, None] * places[None, :] % full_len).astype(jnp.float32)
    phase = residue * (2.0 * math.pi / full_len)
    factor = jnp.ones(mode_ids.shape, jnp.float32)
    if doubled:
        factor = jnp.where(mode_ids == 0, 1.0, 2.0).astype(jnp.float32)
    factor = factor[:, None] / math.sqrt(full_len)
    return jnp.stack([jnp.cos(phase) * factor, -jnp.sin(phase) * factor]).astype(jnp.bfloat16)

def spectral_matrix(filter_weight):
    real_part = filter_weight[0]
    imag_part = filter_weight[1]
    upper_half = jnp.concatenate([real_part, imag_part], axis=1)
    lower_half = jnp.concatenate([-imag_part, real_part], axis=1)
    return jnp.concatenate([upper_half, lower_half], axis=0)

def disco_layer(padded, basis_index, quad_weight, disco_weight, lat_rows, lon_cols):
    basis_count = disco_weight.shape[0]
    groups = disco_weight.shape[1]
    group_ch = disco_weight.shape[2]
    selector = jnp.where(basis_index[:, :, None] == jnp.arange(basis_count, dtype=jnp.int32)[None, None, :], quad_weight[:, :, None], jnp.zeros((), quad_weight.dtype))

    def one_row(row_index):
        lat_band = lax.dynamic_slice_in_dim(padded, row_index, 5, 0)
        windows = jnp.stack([lat_band[lat_off, lon_off:lon_off + lon_cols] for lat_off in range(5) for lon_off in range(5)])
        coeffs = lax.dynamic_index_in_dim(selector, row_index, 0, keepdims=False)
        response = jnp.einsum('pjc,pk->kjc', windows.astype(jnp.float32), coeffs.astype(jnp.float32)).astype(jnp.bfloat16)
        grouped = response.reshape(basis_count, lon_cols, groups, group_ch)
        mixed = jnp.einsum('kjgi,kgio->jgo', grouped.astype(jnp.float32), disco_weight.astype(jnp.float32))
        return mixed.reshape(lon_cols, groups * group_ch).astype(jnp.bfloat16)
    return lax.map(one_row, jnp.arange(lat_rows, dtype=jnp.int32))

def reference(grid_field, basis_index, quad_weight, disco_weight, mode_order, legendre, filter_weight, inner_weight, outer_weight):
    lat_rows, lon_cols, channels = grid_field.shape
    with_poles = jnp.pad(grid_field, ((2, 2), (0, 0), (0, 0)))
    padded = jnp.concatenate([with_poles[:, -2:], with_poles, with_poles[:, :2]], axis=1)
    disco_out = disco_layer(padded, basis_index, quad_weight, disco_weight, lat_rows, lon_cols)
    all_lons = jnp.arange(lon_cols, dtype=jnp.int32)
    forward_tab = twiddle(mode_order, all_lons, lon_cols, False)
    spectra = jnp.einsum('rsl,alc->sarc', forward_tab.astype(jnp.float32), disco_out.astype(jnp.float32)).astype(jnp.bfloat16)
    degrees = legendre.shape[1]
    allowed = jnp.arange(degrees, dtype=jnp.int32)[None, :] >= mode_order[:, None]
    legend_tab = jnp.where(allowed[:, :, None], legendre, jnp.zeros((), legendre.dtype))
    coeffs = jnp.einsum('tla,tarc->tlrc', legend_tab.astype(jnp.float32), spectra.astype(jnp.float32)).astype(jnp.bfloat16)
    filtered = jnp.dot(coeffs.reshape(-1, 2 * channels), spectral_matrix(filter_weight), preferred_element_type=jnp.float32).astype(jnp.bfloat16).reshape(coeffs.shape)
    back_spectra = jnp.einsum('tla,tlrc->tarc', legend_tab.astype(jnp.float32), filtered.astype(jnp.float32)).astype(jnp.bfloat16)
    inverse_tab = twiddle(mode_order, all_lons, lon_cols, True)
    spatial = jnp.einsum('rsl,sarc->alc', inverse_tab.astype(jnp.float32), back_spectra.astype(jnp.float32)).astype(jnp.bfloat16)
    mixed_in = jax.nn.gelu(spatial.astype(jnp.float32) + disco_out.astype(jnp.float32), approximate=True).astype(jnp.bfloat16)
    hidden = jax.nn.gelu(jnp.dot(mixed_in.reshape(-1, channels), inner_weight, preferred_element_type=jnp.float32), approximate=True).astype(jnp.bfloat16)
    result = grid_field.astype(jnp.float32).reshape(-1, channels) + jnp.dot(hidden, outer_weight, preferred_element_type=jnp.float32)
    return result.reshape(lat_rows, lon_cols, channels).astype(jnp.bfloat16)
```

```python
import math

import jax
import jax.numpy as jnp
import numpy as np
from jax import lax
from jax.experimental import pallas as pl
from jax.experimental.pallas import tpu as pltpu
from jax.sharding import PartitionSpec as P

MESH = pl.DeviceIdType.MESH
BF = jnp.bfloat16
F32 = jnp.float32
I32 = jnp.int32

LATS = 64
LONS = 4
NLON = 1024
MODES = 512
ROWS = 8
COLS = 256
CH = 256
HALF = 128
WIN = 96
TILE = 64
RIM = 16


def wave_tables():
    q = (np.arange(MODES)[:, None] * np.arange(NLON)[None, :]) % NLON
    phase = 2.0 * np.pi * q / NLON
    waves = np.stack([np.cos(phase), -np.sin(phase)]) / math.sqrt(NLON)
    return waves


def dot(a, b):
    return jnp.dot(a, b, preferred_element_type=F32)


def gelu(x):
    return jax.nn.gelu(x, approximate=True)


def rows_of(start, size):
    return pl.ds(pl.multiple_of(start, 16), size)


def half_of(index):
    return pl.ds(pl.multiple_of(index * HALF, HALF), HALF)


def swing(k):
    return ((k + 1) // 2) * (2 * (k % 2) - 1)


def layer(
    field, basis, quad, mix_w, keys, modes, legendre, filt, inner, outer, waves, waves_t,
    out,
    ext, wdisco, tab, tab_t, wav, wav_t, band, diag, sel, dsend, full, ssend, srecv, spec, leg, leg_t,
    fmat, ssend2, srecv2, zed, psend, precv, perm_a, perm_at, perm_b, perm_bt, w_in, w_out, w_filt,
    load_sem, halo_send, halo_recv, d_send, d_recv, s_send, s_recv, b_send, b_recv, p_send, p_recv,
):
    lat = lax.axis_index("lat")
    lon = lax.axis_index("lon")
    me = lat * LONS + lon
    lat_y = lat % 4
    lat_xz = lat // 4
    my_h = lon // 2
    my_g = lon % 2
    north = (lat + LATS - 1) % LATS
    south = (lat + 1) % LATS
    west = (lon + LONS - 1) % LONS
    east = (lon + 1) % LONS
    across = (lon + 2) % LONS

    barrier = pltpu.get_barrier_semaphore()

    def greet(n, carry):
        to = (me + swing(n) + 256) % 256
        pl.semaphore_signal(
            barrier, inc=1, device_id=(to // LONS, to % LONS), device_id_type=MESH
        )
        return carry

    lax.fori_loop(1, 256, greet, 0)

    loads = [
        pltpu.make_async_copy(field, ext.at[2 : 2 + ROWS, RIM : RIM + COLS, :], load_sem.at[0]),
        pltpu.make_async_copy(waves, wav, load_sem.at[1]),
        pltpu.make_async_copy(waves_t, wav_t, load_sem.at[2]),
        pltpu.make_async_copy(legendre, leg, load_sem.at[3]),
        pltpu.make_async_copy(inner, w_in, load_sem.at[4]),
        pltpu.make_async_copy(outer, w_out, load_sem.at[5]),
        pltpu.make_async_copy(filt, w_filt, load_sem.at[6]),
    ]
    for load in loads:
        load.start()
    for g in range(2):
        for k in range(4):
            pltpu.make_async_copy(
                mix_w.at[k, g], wdisco.at[g, k * HALF : (k + 1) * HALF, :], load_sem.at[7]
            ).start()

    row = lax.broadcasted_iota(I32, (256, 256), 0)
    col = lax.broadcasted_iota(I32, (256, 256), 1)

    def sent(n):
        return ((n // 4) % 4) * 64 + (n % 2) * 32 + (n // 16) * 2 + (n // 2) % 2

    def gathered(n):
        return ((n % 64) // 4) * 16 + (n % 4) * 4 + (n // 128) * 2 + (n // 64) % 2

    perm_a[...] = (col == sent(row)).astype(F32).astype(BF)
    perm_at[...] = (row == sent(col)).astype(F32).astype(BF)
    perm_b[...] = (col == gathered(row)).astype(F32).astype(BF)
    perm_bt[...] = (row == gathered(col)).astype(F32).astype(BF)

    point = lax.broadcasted_iota(I32, (25, 512), 0)
    lane25 = lax.broadcasted_iota(I32, (25, 512), 1)
    lane8 = lax.broadcasted_iota(I32, (8, 512), 1)
    lat_row = lat * ROWS + lax.broadcasted_iota(I32, (8, 512), 0) + lane8 // WIN - 2
    inside = (lat_row >= 0) & (lat_row < LATS * ROWS) & (lane8 < 5 * WIN)
    quads = quad[...]
    bases = basis[...].astype(F32).astype(BF)
    for dx in range(5):
        pick = (point == 5 * (lane25 // WIN) + dx).astype(F32).astype(BF)
        weight = jnp.where(inside, dot(quads, pick), 0.0)
        kind = dot(bases, pick)
        for k in range(4):
            sel[5 * k + dx] = jnp.where(kind == float(k), weight, 0.0)
    lane64 = lax.broadcasted_iota(I32, (TILE, 512), 1)
    diag[...] = jnp.where(
        lane64 < 5 * WIN,
        lane64 % WIN - (RIM - 2) - lax.broadcasted_iota(I32, (TILE, 512), 0),
        -1000,
    )

    pl.semaphore_wait(barrier, 255)

    top, bottom = slice(0, 2), slice(ROWS - 2, ROWS)
    left, right = slice(0, RIM), slice(COLS - RIM, COLS)
    here_rows, here_cols = slice(2, 2 + ROWS), slice(RIM, RIM + COLS)
    above, below = slice(0, 2), slice(ROWS + 2, ROWS + 4)
    before, after = slice(0, RIM), slice(RIM + COLS, 2 * RIM + COLS)
    whole = slice(None)
    plan = [
        ((south, lon), (bottom, whole), (above, here_cols)),
        ((north, lon), (top, whole), (below, here_cols)),
        ((lat, east), (whole, right), (here_rows, before)),
        ((lat, west), (whole, left), (here_rows, after)),
        ((south, east), (bottom, right), (above, before)),
        ((south, west), (bottom, left), (above, after)),
        ((north, east), (top, right), (below, before)),
        ((north, west), (top, left), (below, after)),
    ]
    rims = []
    for n, (peer, (sr, sc), (dr, dc)) in enumerate(plan):
        rims.append(
            pltpu.make_async_remote_copy(
                field.at[sr, sc, :], ext.at[dr, dc, :], halo_send.at[n], halo_recv.at[n],
                device_id=peer, device_id_type=MESH,
            )
        )
    for rim in rims:
        rim.start()

    key_rows = keys[...].astype(F32)
    key_cols = jnp.transpose(
        jnp.concatenate([key_rows, jnp.zeros((HALF - 8, HALF), F32)], axis=0)
    ).astype(I32)
    loads[1].wait()
    for y in range(4):
        hot = (
            (lax.broadcasted_iota(I32, (HALF, MODES), 1) == key_cols[:, y : y + 1])
            .astype(F32)
            .astype(BF)
        )
        for r in range(2):
            tab[(2 * y + r) * HALF : (2 * y + r + 1) * HALF, :] = dot(hot, wav[r]).astype(BF)

    loads[0].wait()
    pltpu.make_async_copy(wdisco, wdisco, load_sem.at[7]).wait()
    for rim in rims:
        rim.wait()

    def conv_row(a, carry):
        shift = diag[...]
        for k in range(4):
            values = jnp.zeros((TILE, 512), F32)
            for dx in range(5):
                values = jnp.where(shift == dx, sel[5 * k + dx, pl.ds(a, 1), :], values)
            band[k * TILE : (k + 1) * TILE, :] = values.astype(BF)
        parts = [[], []]
        for tile in range(COLS // TILE):
            j = tile * TILE
            window = jnp.concatenate(
                [ext[a + dy, j : j + WIN, :] for dy in range(5)] + [ext[a, j : j + 32, :]], axis=0
            )
            response = dot(band[...], window).astype(BF)
            for g in range(2):
                parts[g].append(
                    jnp.concatenate(
                        [
                            response[k * TILE : (k + 1) * TILE, g * HALF : (g + 1) * HALF]
                            for k in range(4)
                        ],
                        axis=1,
                    )
                )
        for g in range(2):
            mixed = dot(jnp.concatenate(parts[g], axis=0), wdisco[g]).astype(BF)
            dsend[(a // 4) * 2 + g, :, half_of(a % 4)] = mixed
        return carry

    def d_copy(part):
        return pltpu.make_async_remote_copy(
            dsend.at[part], full.at[rows_of(lon * COLS, COLS), :], d_send, d_recv,
            device_id=(lat, part), device_id_type=MESH,
        )

    def d_start(part):
        @pl.when(part != lon)
        def _():
            d_copy(part).start()

        @pl.when(part == lon)
        def _():
            pltpu.make_async_copy(
                dsend.at[part], full.at[rows_of(lon * COLS, COLS), :], d_recv
            ).start()

    lax.fori_loop(0, 4, conv_row, 0)
    d_start(0)
    d_start(1)
    lax.fori_loop(4, 8, conv_row, 0)
    d_start(2)
    d_start(3)

    loads[3].wait()
    for t in range(2):
        least = modes[me * 2 + t]
        allowed = lax.broadcasted_iota(I32, (MODES, MODES), 0) >= least
        masked = jnp.where(allowed, leg[t].astype(F32), 0.0)
        leg[t] = masked.astype(BF)
        leg_t[t] = jnp.transpose(masked).astype(BF)
    loads[6].wait()
    fmat[0:CH, 0:CH] = w_filt[0]
    fmat[0:CH, CH : 2 * CH] = w_filt[1]
    fmat[CH : 2 * CH, 0:CH] = -w_filt[1]
    fmat[CH : 2 * CH, CH : 2 * CH] = w_filt[0]

    pltpu.make_async_copy(full, full, d_recv).wait()
    my_pos = lat_xz * 4 + lon

    def s_block(i, carry):
        y = (lat_y + i) % 4
        waved = dot(tab[rows_of(y * 256, 256), :], full[...]).astype(BF)
        for q in range(4):
            stacked = jnp.concatenate(
                [
                    waved[r * HALF + q * 32 : r * HALF + q * 32 + 32, a * HALF : (a + 1) * HALF]
                    for a in range(4)
                    for r in range(2)
                ],
                axis=0,
            )
            ssend[rows_of((y * 4 + q) * 256, 256), :] = dot(perm_a[...], stacked).astype(BF)

        def one(n, c):
            pos = (my_pos + swing(n) + 64) % 64
            s_copy(y, pos).start()
            return c

        def s_copy(y, pos):
            return pltpu.make_async_remote_copy(
                ssend.at[rows_of((y * 64 + pos) * 16, 16), :],
                srecv.at[rows_of((lat * 2 + my_h) * 16, 16), half_of(my_g)],
                s_send, s_recv,
                device_id=((pos // 4) * 4 + y, pos % 4), device_id_type=MESH,
            )

        @pl.when(i == 0)
        def _():
            pltpu.make_async_copy(
                ssend.at[rows_of((y * 64 + my_pos) * 16, 16), :],
                srecv.at[rows_of((lat * 2 + my_h) * 16, 16), half_of(my_g)],
                s_recv,
            ).start()

        @pl.when(i != 0)
        def _():
            s_copy(y, my_pos).start()

        lax.fori_loop(1, 64, one, 0)
        return carry

    lax.fori_loop(0, 4, s_block, 0)

    loads[2].wait()
    for y in range(4):
        hot = (
            (lax.broadcasted_iota(I32, (MODES, HALF), 0) == keys[y : y + 1, :])
            .astype(F32)
            .astype(BF)
        )
        for r in range(2):
            tab_t[:, (2 * y + r) * HALF : (2 * y + r + 1) * HALF] = dot(wav_t[r], hot).astype(BF)

    pltpu.make_async_copy(srecv, srecv, s_recv).wait()

    for b in range(8):
        turned = dot(perm_b[...], srecv[b * 256 : (b + 1) * 256, :]).astype(BF)
        for t in range(2):
            for r in range(2):
                spec[t, b * 64 : (b + 1) * 64, r * CH : (r + 1) * CH] = turned[
                    t * 128 + r * 64 : t * 128 + r * 64 + 64, :
                ]

    for t in range(2):
        coeffs = dot(leg[t], spec[t]).astype(BF)
        filtered = dot(coeffs, fmat[...]).astype(BF)
        back = dot(leg_t[t], filtered)
        scale = jnp.where(modes[me * 2 + t] == 0, 1.0, 2.0).astype(F32)
        spec[t] = (back * scale).astype(BF)

    for b in range(8):
        stacked = jnp.concatenate(
            [
                spec[t, b * 64 : (b + 1) * 64, r * CH : (r + 1) * CH]
                for t in range(2)
                for r in range(2)
            ],
            axis=0,
        )
        ssend2[b * 256 : (b + 1) * 256, :] = dot(perm_bt[...], stacked).astype(BF)

    back_row = (lat_y * 64 + my_pos) * 16

    def b_one(n, c):
        to = (me + swing(n) + 256) % 256
        pltpu.make_async_remote_copy(
            ssend2.at[rows_of((to // 2) * 16, 16), half_of(to % 2)],
            srecv2.at[rows_of(back_row, 16), :],
            b_send, b_recv,
            device_id=(to // 4, to % 4), device_id_type=MESH,
        ).start()
        return c

    pltpu.make_async_copy(
        ssend2.at[rows_of((me // 2) * 16, 16), half_of(my_g)],
        srecv2.at[rows_of(back_row, 16), :],
        b_recv,
    ).start()
    lax.fori_loop(1, 256, b_one, 0)
    loads[4].wait()
    loads[5].wait()
    pltpu.make_async_copy(srecv2, srecv2, b_recv).wait()

    for n in range(16):
        turned = dot(perm_at[...], srecv2[n * 256 : (n + 1) * 256, :]).astype(BF)
        for a in range(4):
            for r in range(2):
                start = (n // 4) * 256 + r * HALF + (n % 4) * 32
                zed[start : start + 32, a * HALF : (a + 1) * HALF] = turned[
                    a * 64 + r * 32 : a * 64 + r * 32 + 32, :
                ]

    def p_block(i, carry):
        to = (lon + 1 + i) % LONS
        part = rows_of(to * COLS, COLS)
        psend[part, :] = dot(tab_t[part, :], zed[...]).astype(BF)

        @pl.when(i != 3)
        def _():
            pltpu.make_async_remote_copy(
                psend.at[part, :], precv.at[lon], p_send, p_recv,
                device_id=(lat, to), device_id_type=MESH,
            ).start()

        @pl.when(i == 3)
        def _():
            pltpu.make_async_copy(psend.at[part, :], precv.at[lon], p_recv).start()

        return carry

    lax.fori_loop(0, 4, p_block, 0)
    pltpu.make_async_copy(precv, precv, p_recv).wait()

    def mlp_row(a, carry):
        h = a // 4
        lanes = half_of(a % 4)
        mixed = jnp.concatenate(
            [
                gelu(precv[2 * h + g, :, lanes].astype(F32) + dsend[2 * h + g, :, lanes].astype(F32))
                for g in range(2)
            ],
            axis=1,
        ).astype(BF)
        hidden = gelu(dot(mixed, w_in[...])).astype(BF)
        result = ext[a + 2, RIM : RIM + COLS, :].astype(F32) + dot(hidden, w_out[...])
        out[a] = result.astype(BF)
        return carry

    lax.fori_loop(0, 8, mlp_row, 0)

    pltpu.make_async_copy(dsend.at[0:3], dsend.at[0:3], d_send).wait()
    pltpu.make_async_copy(ssend.at[0:4080], ssend.at[0:4080], s_send).wait()
    pltpu.make_async_copy(srecv2.at[0:4080], srecv2.at[0:4080], b_send).wait()
    pltpu.make_async_copy(psend.at[0 : 3 * COLS], psend.at[0 : 3 * COLS], p_send).wait()


def shards(
    grid_field, basis_index, quad_weight, disco_weight, mode_order, legendre, filter_weight,
    inner_weight, outer_weight,
):
    table = wave_tables()
    waves = jnp.asarray(table, BF)
    waves_t = jnp.asarray(np.swapaxes(table, 1, 2), BF)
    keys = mode_order.reshape(16, 4, 8).transpose(1, 0, 2).reshape(4, HALF)
    keys = jnp.concatenate([keys, keys], axis=0)
    vmem = pl.BlockSpec(memory_space=pltpu.VMEM)
    smem = pl.BlockSpec(memory_space=pltpu.SMEM)
    anywhere = pl.BlockSpec(memory_space=pl.ANY)
    dma = pltpu.SemaphoreType.DMA
    scratch = [
        pltpu.VMEM((ROWS + 4, COLS + 2 * RIM, CH), BF),
        pltpu.VMEM((2, 512, HALF), BF),
        pltpu.VMEM((1024, NLON), BF),
        pltpu.VMEM((NLON, 1024), BF),
        pltpu.VMEM((2, MODES, NLON), BF),
        pltpu.VMEM((2, NLON, MODES), BF),
        pltpu.VMEM((4 * TILE, 512), BF),
        pltpu.VMEM((TILE, 512), I32),
        pltpu.VMEM((20, 8, 512), F32),
        pltpu.VMEM((4, COLS, 512), BF),
        pltpu.VMEM((NLON, 512), BF),
        pltpu.VMEM((4096, HALF), BF),
        pltpu.VMEM((2048, CH), BF),
        pltpu.VMEM((2, 512, 512), BF),
        pltpu.VMEM((2, 512, 512), BF),
        pltpu.VMEM((2, 512, 512), BF),
        pltpu.VMEM((512, 512), BF),
        pltpu.VMEM((2048, CH), BF),
        pltpu.VMEM((4096, HALF), BF),
        pltpu.VMEM((1024, 512), BF),
        pltpu.VMEM((NLON, 512), BF),
        pltpu.VMEM((4, COLS, 512), BF),
        pltpu.VMEM((256, 256), BF),
        pltpu.VMEM((256, 256), BF),
        pltpu.VMEM((256, 256), BF),
        pltpu.VMEM((256, 256), BF),
        pltpu.VMEM((CH, 512), BF),
        pltpu.VMEM((512, CH), BF),
        pltpu.VMEM((2, CH, CH), BF),
        dma((8,)),
        dma((8,)),
        dma((8,)),
        dma, dma, dma, dma, dma, dma, dma, dma,
    ]
    return pl.pallas_call(
        layer,
        out_shape=jax.ShapeDtypeStruct((ROWS, COLS, CH), BF),
        in_specs=[
            anywhere, vmem, vmem, anywhere, vmem, smem, anywhere, anywhere, anywhere, anywhere,
            anywhere, anywhere,
        ],
        out_specs=vmem,
        scratch_shapes=scratch,
        compiler_params=pltpu.CompilerParams(
            collective_id=0, has_side_effects=True, vmem_limit_bytes=56 * 1024 * 1024
        ),
        name="layer",
    )(
        grid_field, basis_index, quad_weight, disco_weight, keys, mode_order, legendre,
        filter_weight, inner_weight, outer_weight, waves, waves_t,
    )


def solution(mesh):
    in_specs = (
        P("lat", "lon", None),
        P("lat", None),
        P("lat", None),
        P(),
        P(),
        P(("lat", "lon"), None, None),
        P(),
        P(),
        P(),
    )
    out_specs = P("lat", "lon", None)
    return jax.shard_map(shards, mesh=mesh, in_specs=in_specs, out_specs=out_specs, check_vma=False)
```

```python
import math

import jax
import jax.numpy as jnp
import numpy as np
from jax import lax
from jax.experimental import pallas as pl
from jax.experimental.pallas import tpu as pltpu
from jax.sharding import PartitionSpec as P

MESH = pl.DeviceIdType.MESH
BF = jnp.bfloat16
F32 = jnp.float32
I32 = jnp.int32

LATS = 64
LONS = 4
NLON = 1024
MODES = 512
ROWS = 8
COLS = 256
CH = 256
HALF = 128
WIN = 96
TILE = 64
RIM = 16


def wave_tables():
    q = (np.arange(MODES)[:, None] * np.arange(NLON)[None, :]) % NLON
    phase = 2.0 * np.pi * q / NLON
    waves = np.stack([np.cos(phase), -np.sin(phase)]) / math.sqrt(NLON)
    return waves


def dot(a, b):
    return jnp.dot(a, b, preferred_element_type=F32)


def gelu(x):
    return jax.nn.gelu(x, approximate=True)


def rows_of(start, size):
    return pl.ds(pl.multiple_of(start, 16), size)


def half_of(index):
    return pl.ds(pl.multiple_of(index * HALF, HALF), HALF)


def wrap(value, size):
    value = jnp.where(value >= size, value - size, value)
    return jnp.where(value < 0, value + size, value)


def one_hot(mask):
    return mask.astype(F32).astype(BF)


def iota(shape, dim):
    return lax.broadcasted_iota(I32, shape, dim)


def layer(
    field, basis, quad, mix_w, order, modes, legendre, filt, inner, outer, waves, waves_t,
    out,
    ext, wdisco, tab, tab_t, wav, wav_t, band, diag, sel, dsend, full, ssend, srecv, spec, leg, leg_t,
    fmat, ssend2, srecv2, zed, psend, precv, perm_a, perm_at, perm_b, perm_bt, w_in, w_out, w_filt, rows,
    load_sem, halo_send, halo_recv, d_send, d_recv, s_send, s_recv, b_send, b_recv, p_send, p_recv, o_sem,
):
    lat = lax.axis_index("lat")
    lon = lax.axis_index("lon")
    lat_x = lat // 32
    lat_z = (lat // 4) % 8
    lat_y = lat % 4
    my_h = lon // 2
    my_g = lon % 2
    north = wrap(lat - 1, LATS)
    south = wrap(lat + 1, LATS)
    west = wrap(lon - 1, LONS)
    east = wrap(lon + 1, LONS)
    my_pos = lat_y * 64 + (lat_x * 8 + lat_z) * 4 + lon
    my_src = lat * 2 + my_h

    barrier = pltpu.get_barrier_semaphore()

    def greet(to_lat, to_lon):
        pl.semaphore_signal(barrier, inc=1, device_id=(to_lat, to_lon), device_id_type=MESH)

    def greet_pair(n, carry):
        for to in (wrap(lat + n, LATS), wrap(lat - n, LATS)):
            for to_lon in range(LONS):
                greet(to, to_lon)
        return carry

    for n in range(1, LONS):
        greet(lat, wrap(lon + n, LONS))
    lax.fori_loop(1, LATS // 2, greet_pair, 0)
    for to_lon in range(LONS):
        greet(wrap(lat + LATS // 2, LATS), to_lon)

    loads = [
        pltpu.make_async_copy(field, ext.at[2 : 2 + ROWS, RIM : RIM + COLS, :], load_sem.at[0]),
        pltpu.make_async_copy(waves, wav, load_sem.at[1]),
        pltpu.make_async_copy(waves_t, wav_t, load_sem.at[2]),
        pltpu.make_async_copy(legendre, leg, load_sem.at[3]),
        pltpu.make_async_copy(inner, w_in, load_sem.at[4]),
        pltpu.make_async_copy(outer, w_out, load_sem.at[5]),
        pltpu.make_async_copy(filt, w_filt, load_sem.at[6]),
    ]
    for load in loads:
        load.start()
    for g in range(2):
        for k in range(4):
            pltpu.make_async_copy(
                mix_w.at[k, g], wdisco.at[g, k * HALF : (k + 1) * HALF, :], load_sem.at[7]
            ).start()

    point = iota((25, 512), 0)
    lane25 = iota((25, 512), 1)
    lane8 = iota((8, 512), 1)
    lat_row = lat * ROWS + iota((8, 512), 0) + lane8 // WIN - 2
    inside = (lat_row >= 0) & (lat_row < LATS * ROWS) & (lane8 < 5 * WIN)
    quads = quad[...]
    bases = basis[...].astype(F32).astype(BF)
    for dx in range(5):
        pick = one_hot(point == 5 * (lane25 // WIN) + dx)
        weight = jnp.where(inside, dot(quads, pick), 0.0)
        kind = dot(bases, pick)
        for k in range(4):
            sel[5 * k + dx] = jnp.where(kind == float(k), weight, 0.0)
    lane64 = iota((TILE, 512), 1)
    diag[...] = jnp.where(
        lane64 < 5 * WIN, lane64 % WIN - (RIM - 2) - iota((TILE, 512), 0), -1000
    )

    def band_row(a, carry):
        for piece in range(TILE // 16):
            at = slice(piece * 16, (piece + 1) * 16)
            hits = [diag[at, :] == dx for dx in range(5)]
            for k in range(4):
                values = jnp.zeros((16, 512), F32)
                for dx in range(5):
                    values = jnp.where(hits[dx], sel[5 * k + dx, pl.ds(a, 1), :], values)
                band[a, k * TILE + piece * 16 : k * TILE + (piece + 1) * 16, :] = values.astype(BF)
        return carry

    lax.fori_loop(0, 8, band_row, 0)

    row = iota((256, 256), 0)
    col = iota((256, 256), 1)

    def sent(n):
        return ((n // 4) % 2) * 128 + (n % 2) * 64 + (n // 8) * 2 + (n // 2) % 2

    def gathered(n):
        at = n % 8
        edge = jnp.where((at // 2 == 0) | (at // 2 == 3), 128, 0)
        src = ((n % 64) // 8) * 2 + at // 4
        return edge + src * 8 + (at % 2) * 4 + (n // 128) * 2 + (n // 64) % 2

    perm_a[...] = one_hot(col == sent(row))
    perm_at[...] = one_hot(row == sent(col))
    perm_b[...] = one_hot(col == gathered(row))
    perm_bt[...] = one_hot(row == gathered(col))

    natural = jnp.concatenate([order[...].astype(F32), jnp.zeros((4, HALF), F32)], axis=0)
    high = jnp.floor(natural * 0.5)
    lane_to = iota((HALF, 512), 1)
    stripe = one_hot(
        iota((HALF, 512), 0)
        == ((lane_to % HALF) // 8 % 4) * 32 + (lane_to // HALF) * 8 + lane_to % 8
    )
    spread = 2.0 * dot(high.astype(BF), stripe) + dot((natural - 2.0 * high).astype(BF), stripe)
    from_row = iota((8, 512), 0) == (iota((8, 512), 1) % HALF) // 32
    keys = jnp.sum(jnp.where(from_row, spread, 0.0), axis=0, keepdims=True)
    key_rows = [keys[:, y * HALF : (y + 1) * HALF] for y in range(4)]
    key_cols = jnp.transpose(
        jnp.concatenate(key_rows + [jnp.zeros((HALF - 4, HALF), F32)], axis=0)
    ).astype(I32)

    pl.semaphore_wait(barrier, LATS * LONS - 1)

    top, bottom = slice(0, 2), slice(ROWS - 2, ROWS)
    left, right = slice(0, RIM), slice(COLS - RIM, COLS)
    here_rows, here_cols = slice(2, 2 + ROWS), slice(RIM, RIM + COLS)
    above, below = slice(0, 2), slice(ROWS + 2, ROWS + 4)
    before, after = slice(0, RIM), slice(RIM + COLS, 2 * RIM + COLS)
    whole = slice(None)
    plan = [
        ((lat, east), (whole, right), (here_rows, before)),
        ((lat, west), (whole, left), (here_rows, after)),
        ((south, lon), (bottom, whole), (above, here_cols)),
        ((north, lon), (top, whole), (below, here_cols)),
        ((south, east), (bottom, right), (above, before)),
        ((south, west), (bottom, left), (above, after)),
        ((north, east), (top, right), (below, before)),
        ((north, west), (top, left), (below, after)),
    ]
    rims = []
    for n, (peer, (sr, sc), (dr, dc)) in enumerate(plan):
        rims.append(
            pltpu.make_async_remote_copy(
                field.at[sr, sc, :], ext.at[dr, dc, :], halo_send.at[n], halo_recv.at[n],
                device_id=peer, device_id_type=MESH,
            )
        )
    for rim in rims:
        rim.start()

    loads[1].wait()
    for y in range(4):
        hot = one_hot(iota((HALF, MODES), 1) == key_cols[:, y : y + 1])
        for r in range(2):
            tab[(2 * y + r) * HALF : (2 * y + r + 1) * HALF, :] = dot(hot, wav[r]).astype(BF)

    def conv_row(chunk, n):
        a = n + 2 if chunk == 0 else n + 4 * (n // 2)
        weights = band[a]
        parts = [[], []]
        for tile in range(COLS // TILE):
            j = tile * TILE
            window = jnp.concatenate(
                [ext[a + dy, j : j + WIN, :] for dy in range(5)] + [ext[a + 2, j : j + 32, :]],
                axis=0,
            )
            response = dot(weights, window).astype(BF)
            for g in range(2):
                parts[g].append(
                    jnp.concatenate(
                        [
                            response[k * TILE : (k + 1) * TILE, g * HALF : (g + 1) * HALF]
                            for k in range(4)
                        ],
                        axis=1,
                    )
                )
        for g in range(2):
            mixed = dot(jnp.concatenate(parts[g], axis=0), wdisco[g]).astype(BF)
            dsend[chunk * 4 + (n // 2) * 2 + g, :, half_of(n % 2)] = mixed

    def conv(chunk):
        def body(n, carry):
            conv_row(chunk, n)
            return carry

        lax.fori_loop(0, 4, body, 0)

    far = [(1 - my_h) * 2 + my_g, (1 - my_h) * 2 + 1 - my_g, my_h * 2 + 1 - my_g]
    my_cols = rows_of(lon * COLS, COLS)

    def d_start(chunk):
        for to in far:
            pltpu.make_async_remote_copy(
                dsend.at[chunk * 4 + to], full.at[chunk, my_cols, :], d_send, d_recv.at[chunk],
                device_id=(lat, to), device_id_type=MESH,
            ).start()
        pltpu.make_async_copy(
            dsend.at[chunk * 4 + lon], full.at[chunk, my_cols, :], d_recv.at[chunk]
        ).start()

    loads[0].wait()
    pltpu.make_async_copy(wdisco, wdisco, load_sem.at[7]).wait()
    rims[0].wait()
    rims[1].wait()
    conv(0)
    d_start(0)
    for rim in rims[2:]:
        rim.wait()
    conv(1)
    d_start(1)

    def s_send_all(chunk):
        def step(i, carry):
            y = wrap(lat_y + i, 4)
            waved = dot(tab[rows_of(y * 256, 256), :], full[chunk]).astype(BF)
            for q in range(2):
                stacked = jnp.concatenate(
                    [
                        waved[r * HALF + q * 64 : r * HALF + q * 64 + 64, a * HALF : (a + 1) * HALF]
                        for a in range(2)
                        for r in range(2)
                    ],
                    axis=0,
                )
                block = dot(perm_a[...], stacked).reshape(32, 8, HALF).astype(BF)
                ssend[pl.ds(chunk * 256 + y * 64 + q * 32, 32)] = block

            def source(x, z, to_lon):
                return ssend.at[chunk * 256 + y * 64 + (x * 8 + z) * 4 + to_lon]

            target = srecv.at[chunk * 128 + my_src, :, half_of(my_g)]
            for dz in (4, 3, -3, 2, -2, 1, -1, 0):
                z = wrap(lat_z + dz, 8)
                for dx in (1, 0):
                    x = wrap(lat_x + dx, 2)
                    for dl in (2, 3, 1, 0):
                        to_lon = wrap(lon + dl, LONS)

                        def remote():
                            pltpu.make_async_remote_copy(
                                source(x, z, to_lon), target, s_send, s_recv.at[chunk],
                                device_id=(x * 32 + z * 4 + y, to_lon), device_id_type=MESH,
                            ).start()

                        if dz == 0 and dx == 0 and dl == 0:
                            pl.when(i != 0)(remote)

                            @pl.when(i == 0)
                            def _():
                                pltpu.make_async_copy(
                                    source(x, z, to_lon), target, s_recv.at[chunk]
                                ).start()
                        else:
                            remote()
            return carry

        lax.fori_loop(0, 4, step, 0)

    loads[3].wait()
    for t in range(2):
        least = modes[(lat * LONS + lon) * 2 + t]
        masked = jnp.where(iota((MODES, MODES), 0) >= least, leg[t].astype(F32), 0.0)
        leg[t] = masked.astype(BF)
        leg_t[t] = jnp.transpose(masked).astype(BF)
    loads[6].wait()
    fmat[0:CH, 0:CH] = w_filt[0]
    fmat[0:CH, CH : 2 * CH] = w_filt[1]
    fmat[CH : 2 * CH, 0:CH] = -w_filt[1]
    fmat[CH : 2 * CH, CH : 2 * CH] = w_filt[0]

    for chunk in range(2):
        pltpu.make_async_copy(full.at[chunk], full.at[chunk], d_recv.at[chunk]).wait()
        s_send_all(chunk)

    loads[2].wait()
    for y in range(4):
        hot = one_hot(iota((MODES, HALF), 0) == key_rows[y].astype(I32))
        for r in range(2):
            tab_t[:, (2 * y + r) * HALF : (2 * y + r + 1) * HALF] = dot(wav_t[r], hot).astype(BF)

    for chunk in range(2):
        arrived = srecv.at[chunk * 128 : (chunk + 1) * 128]
        pltpu.make_async_copy(arrived, arrived, s_recv.at[chunk]).wait()

    def flat(block):
        return block.astype(F32).reshape(block.shape[0] * 8, block.shape[2]).astype(BF)

    for b in range(8):
        pair = [flat(srecv[chunk * 128 + b * 16 : chunk * 128 + (b + 1) * 16]) for chunk in range(2)]
        turned = dot(perm_b[...], jnp.concatenate(pair, axis=0)).astype(BF)
        for t in range(2):
            for r in range(2):
                spec[t, b * 64 : (b + 1) * 64, r * CH : (r + 1) * CH] = turned[
                    t * 128 + r * 64 : t * 128 + r * 64 + 64, :
                ]

    for t in range(2):
        coeffs = dot(leg[t], spec[t]).astype(BF)
        filtered = dot(coeffs, fmat[...]).astype(BF)
        back = dot(leg_t[t], filtered)
        scale = jnp.where(modes[(lat * LONS + lon) * 2 + t] == 0, 1.0, 2.0).astype(F32)
        spec[t] = (back * scale).astype(BF)

    for b in range(8):
        stacked = jnp.concatenate(
            [
                spec[t, b * 64 : (b + 1) * 64, r * CH : (r + 1) * CH]
                for t in range(2)
                for r in range(2)
            ],
            axis=0,
        )
        turned = dot(perm_bt[...], stacked)
        for chunk in range(2):
            ssend2[chunk * 128 + b * 16 : chunk * 128 + (b + 1) * 16] = (
                turned[chunk * 128 : (chunk + 1) * 128].reshape(16, 8, CH).astype(BF)
            )

    for chunk in range(2):

        def b_step(i, carry):
            y = wrap(lat_y + i, 4)
            target = srecv2.at[chunk * 256 + my_pos]
            for dz in (4, 3, -3, 2, -2, 1, -1, 0):
                z = wrap(lat_z + dz, 8)
                for dx in (1, 0):
                    x = wrap(lat_x + dx, 2)
                    to_lat = x * 32 + z * 4 + y
                    for to_lon in range(LONS):
                        source = ssend2.at[
                            chunk * 128 + to_lat * 2 + to_lon // 2,
                            :,
                            (to_lon % 2) * HALF : (to_lon % 2 + 1) * HALF,
                        ]

                        def remote():
                            pltpu.make_async_remote_copy(
                                source, target, b_send, b_recv.at[chunk],
                                device_id=(to_lat, to_lon), device_id_type=MESH,
                            ).start()

                        if dz == 0 and dx == 0:
                            own = (i == 0) & (lon == to_lon)
                            pl.when(jnp.logical_not(own))(remote)

                            @pl.when(own)
                            def _():
                                pltpu.make_async_copy(source, target, b_recv.at[chunk]).start()
                        else:
                            remote()
            return carry

        lax.fori_loop(0, 4, b_step, 0)

    loads[4].wait()
    loads[5].wait()

    for chunk in range(2):
        arrived = srecv2.at[chunk * 256 : (chunk + 1) * 256]
        pltpu.make_async_copy(arrived, arrived, b_recv.at[chunk]).wait()
        for q in range(8):
            start = chunk * 256 + q * 32
            turned = dot(perm_at[...], flat(srecv2[start : start + 32])).astype(BF)
            for a in range(2):
                for r in range(2):
                    put = (q // 2) * 256 + r * HALF + (q % 2) * 64
                    zed[chunk, put : put + 64, a * HALF : (a + 1) * HALF] = turned[
                        a * 128 + r * 64 : a * 128 + r * 64 + 64, :
                    ]
        for to in far + [lon]:
            part = rows_of(to * COLS, COLS)
            psend[chunk, part, :] = dot(tab_t[part, :], zed[chunk]).astype(BF)
            target = precv.at[chunk * 4 + lon]
            arrival = p_recv.at[chunk * 2 + my_h]
            if to is lon:
                pltpu.make_async_copy(psend.at[chunk, part, :], target, arrival).start()
            else:
                pltpu.make_async_remote_copy(
                    psend.at[chunk, part, :], target, p_send, arrival,
                    device_id=(lat, to), device_id_type=MESH,
                ).start()

    for chunk in range(2):
        for h in (my_h, 1 - my_h):
            arrived = precv.at[pl.ds(chunk * 4 + 2 * h, 2)]
            pltpu.make_async_copy(arrived, arrived, p_recv.at[chunk * 2 + h]).wait()

            def mlp_row(n, carry, h=h):
                lanes = half_of(n)
                first = chunk * 4 + 2 * h
                mixed = jnp.concatenate(
                    [
                        gelu(
                            precv[first + g, :, lanes].astype(F32)
                            + dsend[first + g, :, lanes].astype(F32)
                        )
                        for g in range(2)
                    ],
                    axis=1,
                ).astype(BF)
                hidden = gelu(dot(mixed, w_in[...])).astype(BF)
                a = 2 + 2 * h + n if chunk == 0 else 6 * h + n
                result = ext[a + 2, RIM : RIM + COLS, :].astype(F32) + dot(hidden, w_out[...])
                rows[a] = result.astype(BF)
                pltpu.make_async_copy(rows.at[a], out.at[a], o_sem).start()
                return carry

            lax.fori_loop(0, 2, mlp_row, 0)

    pltpu.make_async_copy(dsend.at[0:6], dsend.at[0:6], d_send).wait()
    pltpu.make_async_copy(ssend.at[0:510], ssend.at[0:510], s_send).wait()
    pltpu.make_async_copy(srecv2.at[0:510], srecv2.at[0:510], b_send).wait()
    pltpu.make_async_copy(precv.at[0:6], precv.at[0:6], p_send).wait()
    pltpu.make_async_copy(rows, rows, o_sem).wait()


def shards(
    grid_field, basis_index, quad_weight, disco_weight, mode_order, legendre, filter_weight,
    inner_weight, outer_weight,
):
    table = wave_tables()
    waves = jnp.asarray(table, BF)
    waves_t = jnp.asarray(np.swapaxes(table, 1, 2), BF)
    vmem = pl.BlockSpec(memory_space=pltpu.VMEM)
    smem = pl.BlockSpec(memory_space=pltpu.SMEM)
    anywhere = pl.BlockSpec(memory_space=pl.ANY)
    dma = pltpu.SemaphoreType.DMA
    scratch = [
        pltpu.VMEM((ROWS + 4, COLS + 2 * RIM, CH), BF),
        pltpu.VMEM((2, 512, HALF), BF),
        pltpu.VMEM((1024, NLON), BF),
        pltpu.VMEM((NLON, 1024), BF),
        pltpu.VMEM((2, MODES, NLON), BF),
        pltpu.VMEM((2, NLON, MODES), BF),
        pltpu.VMEM((ROWS, 4 * TILE, 512), BF),
        pltpu.VMEM((TILE, 512), I32),
        pltpu.VMEM((20, 8, 512), F32),
        pltpu.VMEM((8, COLS, CH), BF),
        pltpu.VMEM((2, NLON, CH), BF),
        pltpu.VMEM((512, 8, HALF), BF),
        pltpu.VMEM((256, 8, CH), BF),
        pltpu.VMEM((2, 512, 512), BF),
        pltpu.VMEM((2, 512, 512), BF),
        pltpu.VMEM((2, 512, 512), BF),
        pltpu.VMEM((512, 512), BF),
        pltpu.VMEM((256, 8, CH), BF),
        pltpu.VMEM((512, 8, HALF), BF),
        pltpu.VMEM((2, 1024, CH), BF),
        pltpu.VMEM((2, NLON, CH), BF),
        pltpu.VMEM((8, COLS, CH), BF),
        pltpu.VMEM((256, 256), BF),
        pltpu.VMEM((256, 256), BF),
        pltpu.VMEM((256, 256), BF),
        pltpu.VMEM((256, 256), BF),
        pltpu.VMEM((CH, 512), BF),
        pltpu.VMEM((512, CH), BF),
        pltpu.VMEM((2, CH, CH), BF),
        pltpu.VMEM((ROWS, COLS, CH), BF),
        dma((8,)),
        dma((8,)),
        dma((8,)),
        dma,
        dma((2,)),
        dma,
        dma((2,)),
        dma,
        dma((2,)),
        dma,
        dma((4,)),
        dma,
    ]
    return pl.pallas_call(
        layer,
        out_shape=jax.ShapeDtypeStruct((ROWS, COLS, CH), BF),
        in_specs=[
            anywhere, vmem, vmem, anywhere, vmem, smem, anywhere, anywhere, anywhere, anywhere,
            anywhere, anywhere,
        ],
        out_specs=anywhere,
        scratch_shapes=scratch,
        compiler_params=pltpu.CompilerParams(
            collective_id=0, has_side_effects=True, vmem_limit_bytes=56 * 1024 * 1024
        ),
        name="layer",
    )(
        grid_field, basis_index, quad_weight, disco_weight, mode_order.reshape(4, HALF), mode_order,
        legendre, filter_weight, inner_weight, outer_weight, waves, waves_t,
    )


def solution(mesh):
    in_specs = (
        P("lat", "lon", None),
        P("lat", None),
        P("lat", None),
        P(),
        P(),
        P(("lat", "lon"), None, None),
        P(),
        P(),
        P(),
    )
    out_specs = P("lat", "lon", None)
    return jax.shard_map(shards, mesh=mesh, in_specs=in_specs, out_specs=out_specs, check_vma=False)
```

```python
import math

import jax
import jax.numpy as jnp
import numpy as np
from jax import lax
from jax.experimental import pallas as pl
from jax.experimental.pallas import tpu as pltpu
from jax.sharding import PartitionSpec as P

MESH = pl.DeviceIdType.MESH
BF = jnp.bfloat16
F32 = jnp.float32
I32 = jnp.int32

LATS = 64
LONS = 4
NLON = 1024
MODES = 512
ROWS = 8
COLS = 256
CH = 256
HALF = 128
WIN = 96
TILE = 64
RIM = 16


def wave_tables():
    q = (np.arange(MODES)[:, None] * np.arange(NLON)[None, :]) % NLON
    phase = 2.0 * np.pi * q / NLON
    waves = np.stack([np.cos(phase), -np.sin(phase)]) / math.sqrt(NLON)
    return waves


def dot(a, b):
    return jnp.dot(a, b, preferred_element_type=F32)


def gelu(x):
    return jax.nn.gelu(x, approximate=True)


def rows_of(start, size):
    return pl.ds(pl.multiple_of(start, 16), size)


def half_of(index):
    return pl.ds(pl.multiple_of(index * HALF, HALF), HALF)


def wrap(value, size):
    value = jnp.where(value >= size, value - size, value)
    return jnp.where(value < 0, value + size, value)


def one_hot(mask):
    return mask.astype(F32).astype(BF)


def iota(shape, dim):
    return lax.broadcasted_iota(I32, shape, dim)


def layer(
    field, basis, quad, mix_w, order, modes, legendre, filt, inner, outer, waves, waves_t,
    out,
    ext, wdisco, tab, tab_t, wav, wav_t, band, diag, sel, dsend, full, ssend, srecv, spec, leg, leg_t,
    fmat, ssend2, srecv2, zed, acc, psend, precv, perm_a, perm_at, perm_b, perm_bt, w_in, w_out, w_filt, rows, relay,
    load_sem, halo_send, halo_recv, relay_sem, d_send, d_recv, s_send, s_recv, b_send, b_recv, p_send, p_recv, o_sem,
):
    lat = lax.axis_index("lat")
    lon = lax.axis_index("lon")
    lat_x = lat // 32
    lat_z = (lat // 4) % 8
    lat_y = lat % 4
    my_h = lon // 2
    my_g = lon % 2
    north = wrap(lat - 1, LATS)
    south = wrap(lat + 1, LATS)
    west = wrap(lon - 1, LONS)
    east = wrap(lon + 1, LONS)
    my_pos = lat_y * 64 + (lat_x * 8 + lat_z) * 4 + lon
    my_src = lat * 2 + my_h

    barrier = pltpu.get_barrier_semaphore()

    def greet(to_lat, to_lon):
        pl.semaphore_signal(barrier, inc=1, device_id=(to_lat, to_lon), device_id_type=MESH)

    def greet_pair(n, carry):
        for to in (wrap(lat + n, LATS), wrap(lat - n, LATS)):
            for to_lon in range(LONS):
                greet(to, to_lon)
        return carry

    for n in range(1, LONS):
        greet(lat, wrap(lon + n, LONS))
    lax.fori_loop(1, LATS // 2, greet_pair, 0)
    for to_lon in range(LONS):
        greet(wrap(lat + LATS // 2, LATS), to_lon)

    loads = [
        pltpu.make_async_copy(field, ext.at[2 : 2 + ROWS, RIM : RIM + COLS, :], load_sem.at[0]),
        pltpu.make_async_copy(waves, wav, load_sem.at[1]),
        pltpu.make_async_copy(waves_t, wav_t, load_sem.at[2]),
        pltpu.make_async_copy(legendre, leg, load_sem.at[3]),
        pltpu.make_async_copy(inner, w_in, load_sem.at[4]),
        pltpu.make_async_copy(outer, w_out, load_sem.at[5]),
        pltpu.make_async_copy(filt, w_filt, load_sem.at[6]),
    ]
    for load in loads:
        load.start()
    for g in range(2):
        for k in range(4):
            pltpu.make_async_copy(
                mix_w.at[k, g], wdisco.at[g, k * HALF : (k + 1) * HALF, :], load_sem.at[7]
            ).start()

    point = iota((25, 512), 0)
    lane25 = iota((25, 512), 1)
    lane8 = iota((8, 512), 1)
    lat_row = lat * ROWS + iota((8, 512), 0) + lane8 // WIN - 2
    inside = (lat_row >= 0) & (lat_row < LATS * ROWS) & (lane8 < 5 * WIN)
    quads = quad[...]
    bases = basis[...].astype(F32).astype(BF)
    for dx in range(5):
        pick = one_hot(point == 5 * (lane25 // WIN) + dx)
        weight = jnp.where(inside, dot(quads, pick), 0.0)
        kind = dot(bases, pick)
        for k in range(4):
            sel[5 * k + dx] = jnp.where(kind == float(k), weight, 0.0)
    lane64 = iota((TILE, 512), 1)
    diag[...] = jnp.where(
        lane64 < 5 * WIN, lane64 % WIN - (RIM - 2) - iota((TILE, 512), 0), -1000
    )

    def band_row(a, carry):
        for piece in range(TILE // 16):
            at = slice(piece * 16, (piece + 1) * 16)
            hits = [diag[at, :] == dx for dx in range(5)]
            for k in range(4):
                values = jnp.zeros((16, 512), F32)
                for dx in range(5):
                    values = jnp.where(hits[dx], sel[5 * k + dx, pl.ds(a, 1), :], values)
                band[a, k * TILE + piece * 16 : k * TILE + (piece + 1) * 16, :] = values.astype(BF)
        return carry


    def edge_band(n, carry):
        return band_row(jnp.where(n < 2, n, n + 4), carry)

    lax.fori_loop(2, 6, band_row, 0)

    pl.semaphore_wait(barrier, LATS * LONS - 1)

    top, bottom = slice(0, 2), slice(ROWS - 2, ROWS)
    left, right = slice(0, RIM), slice(COLS - RIM, COLS)
    here_rows, here_cols = slice(2, 2 + ROWS), slice(RIM, RIM + COLS)
    above, below = slice(0, 2), slice(ROWS + 2, ROWS + 4)
    before, after = slice(0, RIM), slice(RIM + COLS, 2 * RIM + COLS)
    whole = slice(None)
    plan = [
        ((lat, east), (whole, right), (here_rows, before)),
        ((lat, west), (whole, left), (here_rows, after)),
        ((south, lon), (bottom, whole), (above, here_cols)),
        ((north, lon), (top, whole), (below, here_cols)),
        ((south, east), (bottom, right), (above, before)),
        ((south, west), (bottom, left), (above, after)),
        ((north, east), (top, right), (below, before)),
        ((north, west), (top, left), (below, after)),
    ]
    rims = []
    for n, (peer, (sr, sc), (dr, dc)) in enumerate(plan):
        rims.append(
            pltpu.make_async_remote_copy(
                field.at[sr, sc, :], ext.at[dr, dc, :], halo_send.at[n], halo_recv.at[n],
                device_id=peer, device_id_type=MESH,
            )
        )
    for rim in rims[:2]:
        rim.start()
    for n in (2, 4, 5):
        pl.when((lat != LATS - 1) if n > 2 else (lat != LATS - 1) & (lat != 31))(rims[n].start)
    for n in (3, 6, 7):
        pl.when((lat != 0) if n > 3 else (lat != 0) & (lat != 32))(rims[n].start)

    quarter = COLS // 4

    def pieces(n, source_rows, target_rows, direct, peer, first_relay):
        for p in range(4):
            cols = slice(p * quarter, (p + 1) * quarter)
            if p == direct:
                put = ext.at[target_rows, RIM + p * quarter : RIM + (p + 1) * quarter, :]
            pltpu.make_async_remote_copy(
                field.at[source_rows, cols, :],
                put if p == direct else relay,
                halo_send.at[n],
                halo_recv.at[n] if p == direct else relay_sem.at[0],
                device_id=(peer if p == direct else first_relay + p, lon), device_id_type=MESH,
            ).start()

    @pl.when(lat == 31)
    def _():
        pieces(2, bottom, above, 3, 32, 0)

    @pl.when(lat == 32)
    def _():
        pieces(3, top, below, 0, 31, 60)

    def forward(n, target_rows, p, peer):
        put = ext.at[target_rows, rows_of(RIM + p * quarter, quarter), :]
        pltpu.make_async_copy(relay, relay, relay_sem.at[0]).wait()
        pltpu.make_async_remote_copy(
            relay, put, relay_sem.at[1], halo_recv.at[n],
            device_id=(peer, lon), device_id_type=MESH,
        ).start()

    def forward_rows():
        pl.when(lat < 3)(lambda: forward(2, above, lat, 32))
        pl.when(lat > 60)(lambda: forward(3, below, lat - 60, 31))

    def wait_rows():
        for n in (2, 4, 5):
            pl.when(lat != LATS - 1)(rims[n].wait_send)
            pl.when(lat != 0)(rims[n].wait_recv)
        for n in (3, 6, 7):
            pl.when(lat != 0)(rims[n].wait_send)
            pl.when(lat != LATS - 1)(rims[n].wait_recv)

    @pl.when(lat == 0)
    def _():
        ext[above] = jnp.zeros((2, COLS + 2 * RIM, CH), BF)

    @pl.when(lat == LATS - 1)
    def _():
        ext[below] = jnp.zeros((2, COLS + 2 * RIM, CH), BF)

    far_h = 1 - my_h
    my_cols = rows_of(lon * COLS, COLS)

    def row_of(c, h):
        return jnp.where(h == 0, 3 - c, 4 + c)

    def conv(c, tiles):
        done = []
        for h in (far_h, my_h):
            a = row_of(c, h)
            weights = band[a]
            parts = [[], []]
            for tile in tiles:
                j = tile * TILE
                window = jnp.concatenate(
                    [ext[a + dy, j : j + WIN, :] for dy in range(5)] + [ext[a + 2, j : j + 32, :]],
                    axis=0,
                )
                response = dot(weights, window).astype(BF)
                for g in range(2):
                    parts[g].append(
                        jnp.concatenate(
                            [
                                response[k * TILE : (k + 1) * TILE, g * HALF : (g + 1) * HALF]
                                for k in range(4)
                            ],
                            axis=1,
                        )
                    )
            done.append(parts)
        for h, parts in zip((far_h, my_h), done):
            for g in range(2):
                mixed = dot(jnp.concatenate(parts[g], axis=0), wdisco[g]).astype(BF)
                for n, tile in enumerate(tiles):
                    dsend[c * 4 + 2 * h + g, tile * TILE : (tile + 1) * TILE, :] = mixed[
                        n * TILE : (n + 1) * TILE, :
                    ]

    def d_start(c):
        target = full.at[my_cols, c * HALF : (c + 1) * HALF]
        for to in (far_h * 2 + my_g, far_h * 2 + 1 - my_g, my_h * 2 + 1 - my_g):
            pltpu.make_async_remote_copy(
                dsend.at[c * 4 + to], target, d_send, d_recv.at[c],
                device_id=(lat, to), device_id_type=MESH,
            ).start()
        pltpu.make_async_copy(dsend.at[c * 4 + lon], target, d_recv.at[c]).start()

    def d_wait(c):
        arrived = full.at[:, c * HALF : (c + 1) * HALF]
        pltpu.make_async_copy(arrived, arrived, d_recv.at[c]).wait()

    loads[0].wait()
    pltpu.make_async_copy(wdisco, wdisco, load_sem.at[7]).wait()
    conv(0, (1, 2))
    conv(1, (1, 2))

    row = iota((256, 256), 0)
    col = iota((256, 256), 1)

    def paired(n):
        return (n % 2) * 128 + n // 2

    def gathered(n):
        at = n % 8
        place = jnp.where(at < 4, 3 - at, at)
        return ((n % 128) // 8) * 16 + place * 2 + n // 128

    perm_a[...] = one_hot(col == paired(row))
    perm_at[...] = one_hot(row == paired(col))
    perm_b[...] = one_hot(col == gathered(row))
    perm_bt[...] = one_hot(row == gathered(col))

    natural = jnp.concatenate([order[...].astype(F32), jnp.zeros((4, HALF), F32)], axis=0)
    high = jnp.floor(natural * 0.5)
    lane_to = iota((HALF, 512), 1)
    stripe = one_hot(
        iota((HALF, 512), 0)
        == (lane_to // 4 % 4) * 32 + (lane_to // 64 % 4) * 8 + (lane_to % 4) * 2 + lane_to // 256
    )
    spread = 2.0 * dot(high.astype(BF), stripe) + dot((natural - 2.0 * high).astype(BF), stripe)
    from_row = iota((8, 512), 0) == iota((8, 512), 1) // 16 % 4
    keys = jnp.sum(jnp.where(from_row, spread, 0.0), axis=0, keepdims=True)
    key_rows = [keys[:, n * HALF : (n + 1) * HALF] for n in range(4)]
    key_cols = jnp.transpose(
        jnp.concatenate(key_rows + [jnp.zeros((HALF - 4, HALF), F32)], axis=0)
    ).astype(I32)

    lax.fori_loop(0, 4, edge_band, 0)
    rims[0].wait()
    rims[1].wait()
    conv(0, (0, 3))
    d_start(0)
    conv(1, (0, 3))
    d_start(1)

    loads[1].wait()
    for n in range(4):
        hot = one_hot(iota((HALF, MODES), 1) == key_cols[:, n : n + 1])
        both = jnp.concatenate([dot(hot, wav[r]).astype(BF) for r in range(2)], axis=0)
        tab[n * 256 : (n + 1) * 256, :] = dot(perm_a[...], both).astype(BF)

    def each_device(remote, local):
        def step(i, carry):
            y = wrap(lat_y + i, 4)
            for dz in (4, 3, -3, 2, -2, 1, -1, 0):
                z = wrap(lat_z + dz, 8)
                for dx in (1, 0):
                    x = wrap(lat_x + dx, 2)
                    xz = x * 8 + z
                    for h, g in ((far_h, my_g), (far_h, 1 - my_g), (my_h, 1 - my_g), (my_h, my_g)):
                        peer = (xz * 4 + y, h, g, y * 64 + xz * 4 + 2 * h + g)
                        if dz == 0 and dx == 0 and h is my_h and g is my_g:
                            pl.when(i != 0)(lambda: remote(*peer))
                            pl.when(i == 0)(lambda: local(*peer))
                        else:
                            remote(*peer)
            return carry

        lax.fori_loop(0, 4, step, 0)

    def s_send_blocks(t, first, last):
        target = srecv.at[t * 256 + my_g * 128 + my_src, first:last]
        arrival = s_recv.at[t]

        def remote(to_lat, h, g, pos):
            pltpu.make_async_remote_copy(
                ssend.at[t * 256 + pos, first:last], target, s_send, arrival,
                device_id=(to_lat, 2 * h + g), device_id_type=MESH,
            ).start()

        def local(to_lat, h, g, pos):
            pltpu.make_async_copy(ssend.at[t * 256 + pos, first:last], target, arrival).start()

        each_device(remote, local)

    def wave(t, first, last):
        waved = dot(tab[t * 512 : (t + 1) * 512, :], full[:, first * HALF : last * HALF])
        for c in range(first, last):
            at = (c - first) * HALF
            ssend[t * 256 : (t + 1) * 256, c] = (
                waved[:, at : at + HALF].reshape(256, 2, HALF).astype(BF)
            )

    forward_rows()
    wait_rows()
    for c in (2, 3):
        conv(c, (0, 1, 2, 3))
        d_start(c)
    d_wait(0)
    wave(0, 0, 1)
    s_send_blocks(0, 0, 1)
    d_wait(1)
    wave(0, 1, 2)
    s_send_blocks(0, 1, 2)

    loads[3].wait()
    for t in range(2):
        least = modes[(lat * LONS + lon) * 2 + t]
        masked = jnp.where(iota((MODES, MODES), 0) >= least, leg[t].astype(F32), 0.0)
        leg[t] = masked.astype(BF)
        leg_t[t] = jnp.transpose(masked).astype(BF)
    loads[6].wait()
    fmat[0:CH, 0:CH] = w_filt[0]
    fmat[0:CH, CH : 2 * CH] = w_filt[1]
    fmat[CH : 2 * CH, 0:CH] = -w_filt[1]
    fmat[CH : 2 * CH, CH : 2 * CH] = w_filt[0]

    d_wait(2)
    d_wait(3)
    wave(0, 2, 4)
    s_send_blocks(0, 2, 4)
    wave(1, 0, 4)
    s_send_blocks(1, 0, 4)

    loads[2].wait()
    for n in range(4):
        hot = one_hot(iota((MODES, HALF), 0) == key_rows[n].astype(I32))
        both = jnp.concatenate([dot(wav_t[r], hot).astype(BF) for r in range(2)], axis=1)
        tab_t[:, n * 256 : (n + 1) * 256] = dot(both, perm_at[...]).astype(BF)

    def b_send_blocks(t, first, last, arrival):
        target = srecv2.at[t * 256 + my_pos, first:last]

        def source(to_lat, h, g):
            return ssend2.at[t * 256 + g * 128 + to_lat * 2 + h, first:last]

        def remote(to_lat, h, g, pos):
            pltpu.make_async_remote_copy(
                source(to_lat, h, g), target, b_send, arrival,
                device_id=(to_lat, 2 * h + g), device_id_type=MESH,
            ).start()

        def local(to_lat, h, g, pos):
            pltpu.make_async_copy(source(to_lat, h, g), target, arrival).start()

        each_device(remote, local)

    cuts = ((0, 1), (1, 2), (2, 3), (3, 4))
    for t in range(2):
        arrived = srecv.at[t * 256 : (t + 1) * 256]
        pltpu.make_async_copy(arrived, arrived, s_recv.at[t]).wait()
        for b in range(4):
            sides = [
                srecv[t * 256 + g * 128 + b * 32 : t * 256 + g * 128 + (b + 1) * 32].reshape(
                    256, HALF
                )
                for g in range(2)
            ]
            turned = dot(perm_b[...], jnp.concatenate(sides, axis=1)).astype(BF)
            for r in range(2):
                spec[b * 128 : (b + 1) * 128, r * CH : (r + 1) * CH] = turned[
                    r * 128 : (r + 1) * 128, :
                ]
        coeffs = dot(leg[t], spec[...]).astype(BF)
        filtered = dot(coeffs, fmat[...]).astype(BF)
        back = dot(leg_t[t], filtered)
        scale = jnp.where(modes[(lat * LONS + lon) * 2 + t] == 0, 1.0, 2.0).astype(F32)
        spec[...] = (back * scale).astype(BF)
        for b in range(4):
            stacked = jnp.concatenate(
                [spec[b * 128 : (b + 1) * 128, r * CH : (r + 1) * CH] for r in range(2)], axis=0
            )
            turned = dot(perm_bt[...], stacked)
            for g in range(2):
                ssend2[t * 256 + g * 128 + b * 32 : t * 256 + g * 128 + (b + 1) * 32] = (
                    turned[:, g * HALF : (g + 1) * HALF].reshape(32, 4, 2, HALF).astype(BF)
                )
        if t == 0:
            b_send_blocks(0, 0, 4, b_recv.at[0])
        else:
            for n, (first, last) in enumerate(cuts):
                b_send_blocks(1, first, last, b_recv.at[1 + n])

    loads[4].wait()
    loads[5].wait()

    def unpack(t, first, last):
        for c in range(first, last):
            zed[t, :, c * HALF : (c + 1) * HALF] = srecv2[t * 256 : (t + 1) * 256, c].reshape(
                512, HALF
            )

    arrived = srecv2.at[0:256]
    pltpu.make_async_copy(arrived, arrived, b_recv.at[0]).wait()
    unpack(0, 0, 4)

    def first_half(n, carry):
        part = rows_of(n * 256, 256)
        acc[part, :] = dot(tab_t[part, 0:512], zed[0])
        return carry

    lax.fori_loop(0, 4, first_half, 0)

    near = my_h * 2 + 1 - my_g
    for n, (first, last) in enumerate(cuts):
        arrived = srecv2.at[256:512, first:last]
        pltpu.make_async_copy(arrived, arrived, b_recv.at[1 + n]).wait()
        unpack(1, first, last)
        for c in range(first, last):
            lanes = slice(c * HALF, (c + 1) * HALF)
            target = precv.at[c * 4 + lon]
            arrival = p_recv.at[c * 2 + my_h]
            for to in (far_h * 2 + my_g, far_h * 2 + 1 - my_g, near, lon):
                part = rows_of(to * COLS, COLS)
                total = acc[part, lanes] + dot(tab_t[part, 512:1024], zed[1, :, lanes])
                psend[c, part, :] = total.astype(BF)
                if to is lon:
                    pltpu.make_async_copy(psend.at[c, part, :], target, arrival).start()
                else:
                    pltpu.make_async_remote_copy(
                        psend.at[c, part, :], target, p_send, arrival,
                        device_id=(lat, to), device_id_type=MESH,
                    ).start()

    def mlp(c, carry):
        for h in (my_h, far_h):
            first = c * 4 + 2 * h
            arrived = precv.at[pl.ds(first, 2)]
            pltpu.make_async_copy(arrived, arrived, p_recv.at[c * 2 + h]).wait()
            mixed = jnp.concatenate(
                [
                    gelu(precv[first + g].astype(F32) + dsend[first + g].astype(F32))
                    for g in range(2)
                ],
                axis=1,
            ).astype(BF)
            hidden = gelu(dot(mixed, w_in[...])).astype(BF)
            a = row_of(c, h)
            result = ext[a + 2, RIM : RIM + COLS, :].astype(F32) + dot(hidden, w_out[...])
            rows[a] = result.astype(BF)
            pltpu.make_async_copy(rows.at[a], out.at[a], o_sem).start()
        return carry

    lax.fori_loop(0, 4, mlp, 0)

    @pl.when((lat < 3) | (lat > 60))
    def _():
        pltpu.make_async_copy(relay, relay, relay_sem.at[1]).wait()

    pltpu.make_async_copy(dsend.at[0:12], dsend.at[0:12], d_send).wait()
    pltpu.make_async_copy(ssend.at[0:510], ssend.at[0:510], s_send).wait()
    pltpu.make_async_copy(ssend2.at[0:510], ssend2.at[0:510], b_send).wait()
    pltpu.make_async_copy(precv.at[0:12], precv.at[0:12], p_send).wait()
    pltpu.make_async_copy(rows, rows, o_sem).wait()


def shards(
    grid_field, basis_index, quad_weight, disco_weight, mode_order, legendre, filter_weight,
    inner_weight, outer_weight,
):
    table = wave_tables()
    waves = jnp.asarray(table, BF)
    waves_t = jnp.asarray(np.swapaxes(table, 1, 2), BF)
    vmem = pl.BlockSpec(memory_space=pltpu.VMEM)
    smem = pl.BlockSpec(memory_space=pltpu.SMEM)
    anywhere = pl.BlockSpec(memory_space=pl.ANY)
    hbm = pl.BlockSpec(memory_space=pltpu.HBM)
    dma = pltpu.SemaphoreType.DMA
    scratch = [
        pltpu.VMEM((ROWS + 4, COLS + 2 * RIM, CH), BF),
        pltpu.VMEM((2, 512, HALF), BF),
        pltpu.VMEM((1024, NLON), BF),
        pltpu.VMEM((NLON, 1024), BF),
        pltpu.VMEM((2, MODES, NLON), BF),
        pltpu.VMEM((2, NLON, MODES), BF),
        pltpu.VMEM((ROWS, 4 * TILE, 512), BF),
        pltpu.VMEM((TILE, 512), I32),
        pltpu.VMEM((20, 8, 512), F32),
        pltpu.VMEM((16, COLS, HALF), BF),
        pltpu.VMEM((NLON, 512), BF),
        pltpu.VMEM((512, 4, 2, HALF), BF),
        pltpu.VMEM((512, 4, 2, HALF), BF),
        pltpu.VMEM((512, 512), BF),
        pltpu.VMEM((2, 512, 512), BF),
        pltpu.VMEM((2, 512, 512), BF),
        pltpu.VMEM((512, 512), BF),
        pltpu.VMEM((512, 4, 2, HALF), BF),
        pltpu.VMEM((512, 4, 2, HALF), BF),
        pltpu.VMEM((2, 512, 512), BF),
        pltpu.VMEM((NLON, 512), F32),
        pltpu.VMEM((4, NLON, HALF), BF),
        pltpu.VMEM((16, COLS, HALF), BF),
        pltpu.VMEM((256, 256), BF),
        pltpu.VMEM((256, 256), BF),
        pltpu.VMEM((256, 256), BF),
        pltpu.VMEM((256, 256), BF),
        pltpu.VMEM((CH, 512), BF),
        pltpu.VMEM((512, CH), BF),
        pltpu.VMEM((2, CH, CH), BF),
        pltpu.VMEM((ROWS, COLS, CH), BF),
        pltpu.VMEM((2, COLS // 4, CH), BF),
        dma((8,)),
        dma((8,)),
        dma((8,)),
        dma((2,)),
        dma,
        dma((4,)),
        dma,
        dma((2,)),
        dma,
        dma((5,)),
        dma,
        dma((8,)),
        dma,
    ]
    return pl.pallas_call(
        layer,
        out_shape=jax.ShapeDtypeStruct((ROWS, COLS, CH), BF),
        in_specs=[
            hbm, vmem, vmem, hbm, vmem, smem, hbm, hbm, hbm, hbm,
            hbm, hbm,
        ],
        out_specs=anywhere,
        scratch_shapes=scratch,
        compiler_params=pltpu.CompilerParams(
            collective_id=0, has_side_effects=True, vmem_limit_bytes=56 * 1024 * 1024
        ),
        name="layer",
    )(
        grid_field, basis_index, quad_weight, disco_weight, mode_order.reshape(4, HALF), mode_order,
        legendre, filter_weight, inner_weight, outer_weight, waves, waves_t,
    )


def solution(mesh):
    in_specs = (
        P("lat", "lon", None),
        P("lat", None),
        P("lat", None),
        P(),
        P(),
        P(("lat", "lon"), None, None),
        P(),
        P(),
        P(),
    )
    out_specs = P("lat", "lon", None)
    return jax.shard_map(shards, mesh=mesh, in_specs=in_specs, out_specs=out_specs, check_vma=False)
```

```python
import math

import jax
import jax.numpy as jnp
import numpy as np
from jax import lax
from jax.experimental import pallas as pl
from jax.experimental.pallas import tpu as pltpu
from jax.sharding import PartitionSpec as P

MESH = pl.DeviceIdType.MESH
BF = jnp.bfloat16
F32 = jnp.float32
I32 = jnp.int32

LATS = 64
LONS = 4
NLON = 1024
MODES = 512
ROWS = 8
COLS = 256
CH = 256
HALF = 128
WIN = 96
TILE = 64
RIM = 16


def wave_tables():
    q = (np.arange(MODES)[:, None] * np.arange(NLON)[None, :]) % NLON
    phase = 2.0 * np.pi * q / NLON
    waves = np.stack([np.cos(phase), -np.sin(phase)]) / math.sqrt(NLON)
    return waves


def dot(a, b):
    return jnp.dot(a, b, preferred_element_type=F32)


def gelu(x):
    return jax.nn.gelu(x, approximate=True)


def rows_of(start, size):
    return pl.ds(pl.multiple_of(start, 16), size)


def half_of(index):
    return pl.ds(pl.multiple_of(index * HALF, HALF), HALF)


def wrap(value, size):
    value = jnp.where(value >= size, value - size, value)
    return jnp.where(value < 0, value + size, value)


def one_hot(mask):
    return mask.astype(F32).astype(BF)


def iota(shape, dim):
    return lax.broadcasted_iota(I32, shape, dim)


def layer(
    field, basis, quad, mix_w, order, modes, legendre, filt, inner, outer, waves, waves_t,
    out,
    ext, wdisco, tab, tab_t, wav, wav_t, band, diag, sel, dsend, full, ssend, srecv, spec, leg, leg_t,
    fmat, ssend2, srecv2, zed, acc, psend, precv, perm_a, perm_at, perm_b, perm_bt, w_in, w_out, w_filt, rows, relay,
    load_sem, halo_send, halo_recv, relay_sem, d_send, d_recv, s_send, s_recv, b_send, b_recv, p_send, p_recv, o_sem,
):
    lat = lax.axis_index("lat")
    lon = lax.axis_index("lon")
    lat_x = lat // 32
    lat_z = (lat // 4) % 8
    lat_y = lat % 4
    my_h = lon // 2
    my_g = lon % 2
    north = wrap(lat - 1, LATS)
    south = wrap(lat + 1, LATS)
    west = wrap(lon - 1, LONS)
    east = wrap(lon + 1, LONS)
    my_pos = lat_y * 64 + (lat_x * 8 + lat_z) * 4 + lon
    my_src = lat * 2 + my_h

    barrier = pltpu.get_barrier_semaphore()

    def greet(to_lat, to_lon):
        pl.semaphore_signal(barrier, inc=1, device_id=(to_lat, to_lon), device_id_type=MESH)

    def greet_pair(n, carry):
        for to in (wrap(lat + n, LATS), wrap(lat - n, LATS)):
            for to_lon in range(LONS):
                greet(to, to_lon)
        return carry

    for n in range(1, LONS):
        greet(lat, wrap(lon + n, LONS))
    lax.fori_loop(1, LATS // 2, greet_pair, 0)
    for to_lon in range(LONS):
        greet(wrap(lat + LATS // 2, LATS), to_lon)

    loads = [
        pltpu.make_async_copy(field, ext.at[2 : 2 + ROWS, RIM : RIM + COLS, :], load_sem.at[0]),
        pltpu.make_async_copy(waves, wav, load_sem.at[1]),
        pltpu.make_async_copy(waves_t, wav_t, load_sem.at[2]),
        pltpu.make_async_copy(legendre, leg, load_sem.at[3]),
        pltpu.make_async_copy(inner, w_in, load_sem.at[4]),
        pltpu.make_async_copy(outer, w_out, load_sem.at[5]),
        pltpu.make_async_copy(filt, w_filt, load_sem.at[6]),
    ]
    for load in loads:
        load.start()
    for g in range(2):
        for k in range(4):
            pltpu.make_async_copy(
                mix_w.at[k, g], wdisco.at[g, k * HALF : (k + 1) * HALF, :], load_sem.at[7]
            ).start()

    point = iota((25, 512), 0)
    lane25 = iota((25, 512), 1)
    lane8 = iota((8, 512), 1)
    lat_row = lat * ROWS + iota((8, 512), 0) + lane8 // WIN - 2
    inside = (lat_row >= 0) & (lat_row < LATS * ROWS) & (lane8 < 5 * WIN)
    quads = quad[...]
    bases = basis[...].astype(F32).astype(BF)
    for dx in range(5):
        pick = one_hot(point == 5 * (lane25 // WIN) + dx)
        weight = jnp.where(inside, dot(quads, pick), 0.0)
        kind = dot(bases, pick)
        for k in range(4):
            sel[5 * k + dx] = jnp.where(kind == float(k), weight, 0.0)
    lane64 = iota((TILE, 512), 1)
    diag[...] = jnp.where(
        lane64 < 5 * WIN, lane64 % WIN - (RIM - 2) - iota((TILE, 512), 0), -1000
    )

    def band_row(a, carry):
        for piece in range(TILE // 16):
            at = slice(piece * 16, (piece + 1) * 16)
            hits = [diag[at, :] == dx for dx in range(5)]
            for k in range(4):
                values = jnp.zeros((16, 512), F32)
                for dx in range(5):
                    values = jnp.where(hits[dx], sel[5 * k + dx, pl.ds(a, 1), :], values)
                band[a, k * TILE + piece * 16 : k * TILE + (piece + 1) * 16, :] = values.astype(BF)
        return carry


    def edge_band(n, carry):
        return band_row(jnp.where(n < 2, n, n + 4), carry)

    lax.fori_loop(2, 6, band_row, 0)

    pl.semaphore_wait(barrier, LATS * LONS - 1)

    top, bottom = slice(0, 2), slice(ROWS - 2, ROWS)
    left, right = slice(0, RIM), slice(COLS - RIM, COLS)
    here_rows, here_cols = slice(2, 2 + ROWS), slice(RIM, RIM + COLS)
    above, below = slice(0, 2), slice(ROWS + 2, ROWS + 4)
    before, after = slice(0, RIM), slice(RIM + COLS, 2 * RIM + COLS)
    whole = slice(None)
    plan = [
        ((lat, east), (whole, right), (here_rows, before)),
        ((lat, west), (whole, left), (here_rows, after)),
        ((south, lon), (bottom, whole), (above, here_cols)),
        ((north, lon), (top, whole), (below, here_cols)),
        ((south, east), (bottom, right), (above, before)),
        ((south, west), (bottom, left), (above, after)),
        ((north, east), (top, right), (below, before)),
        ((north, west), (top, left), (below, after)),
    ]
    rims = []
    for n, (peer, (sr, sc), (dr, dc)) in enumerate(plan):
        rims.append(
            pltpu.make_async_remote_copy(
                field.at[sr, sc, :], ext.at[dr, dc, :], halo_send.at[n], halo_recv.at[n],
                device_id=peer, device_id_type=MESH,
            )
        )
    for rim in rims[:2]:
        rim.start()
    for n in (2, 4, 5):
        pl.when((lat != LATS - 1) if n > 2 else (lat != LATS - 1) & (lat != 31))(rims[n].start)
    for n in (3, 6, 7):
        pl.when((lat != 0) if n > 3 else (lat != 0) & (lat != 32))(rims[n].start)

    ways = ((0, HALF), (HALF, HALF))

    def pieces(n, source_rows, target_rows, peer, relays):
        for (start, width), to in zip(ways, (peer,) + relays):
            put = ext.at[target_rows, RIM + start : RIM + start + width, :]
            pltpu.make_async_remote_copy(
                field.at[source_rows, start : start + width, :],
                put if to == peer else relay,
                halo_send.at[n],
                halo_recv.at[n] if to == peer else relay_sem.at[0],
                device_id=(to, lon), device_id_type=MESH,
            ).start()

    @pl.when(lat == 31)
    def _():
        pieces(2, bottom, above, 32, (63,))

    @pl.when(lat == 32)
    def _():
        pieces(3, top, below, 31, (0,))

    def forward(n, target_rows, way, peer):
        start, width = ways[way]
        pltpu.make_async_copy(relay, relay, relay_sem.at[0]).wait()
        pltpu.make_async_remote_copy(
            relay, ext.at[target_rows, RIM + start : RIM + start + width, :],
            relay_sem.at[1], halo_recv.at[n],
            device_id=(peer, lon), device_id_type=MESH,
        ).start()

    def forward_rows():
        pl.when(lat == 63)(lambda: forward(2, above, 1, 32))
        pl.when(lat == 0)(lambda: forward(3, below, 1, 31))

    def wait_rows():
        for n in (2, 4, 5):
            pl.when(lat != LATS - 1)(rims[n].wait_send)
            pl.when(lat != 0)(rims[n].wait_recv)
        for n in (3, 6, 7):
            pl.when(lat != 0)(rims[n].wait_send)
            pl.when(lat != LATS - 1)(rims[n].wait_recv)

    @pl.when(lat == 0)
    def _():
        ext[above] = jnp.zeros((2, COLS + 2 * RIM, CH), BF)

    @pl.when(lat == LATS - 1)
    def _():
        ext[below] = jnp.zeros((2, COLS + 2 * RIM, CH), BF)

    far_h = 1 - my_h
    my_cols = rows_of(lon * COLS, COLS)

    def row_of(c, h):
        return jnp.where(h == 0, 3 - c, 4 + c)

    def conv(c, tiles):
        done = []
        for h in (far_h, my_h):
            a = row_of(c, h)
            weights = band[a]
            parts = [[], []]
            for tile in tiles:
                j = tile * TILE
                window = jnp.concatenate(
                    [ext[a + dy, j : j + WIN, :] for dy in range(5)] + [ext[a + 2, j : j + 32, :]],
                    axis=0,
                )
                response = dot(weights, window).astype(BF)
                for g in range(2):
                    parts[g].append(
                        jnp.concatenate(
                            [
                                response[k * TILE : (k + 1) * TILE, g * HALF : (g + 1) * HALF]
                                for k in range(4)
                            ],
                            axis=1,
                        )
                    )
            done.append(parts)
        for h, parts in zip((far_h, my_h), done):
            for g in range(2):
                mixed = dot(jnp.concatenate(parts[g], axis=0), wdisco[g]).astype(BF)
                for n, tile in enumerate(tiles):
                    dsend[c * 4 + 2 * h + g, tile * TILE : (tile + 1) * TILE, :] = mixed[
                        n * TILE : (n + 1) * TILE, :
                    ]

    def d_start(c):
        target = full.at[my_cols, c * HALF : (c + 1) * HALF]
        for to in (far_h * 2 + my_g, far_h * 2 + 1 - my_g, my_h * 2 + 1 - my_g):
            pltpu.make_async_remote_copy(
                dsend.at[c * 4 + to], target, d_send, d_recv.at[c],
                device_id=(lat, to), device_id_type=MESH,
            ).start()
        pltpu.make_async_copy(dsend.at[c * 4 + lon], target, d_recv.at[c]).start()

    def d_wait(c):
        arrived = full.at[:, c * HALF : (c + 1) * HALF]
        pltpu.make_async_copy(arrived, arrived, d_recv.at[c]).wait()

    loads[0].wait()
    pltpu.make_async_copy(wdisco, wdisco, load_sem.at[7]).wait()
    conv(0, (1, 2))
    conv(1, (1, 2))

    row = iota((256, 256), 0)
    col = iota((256, 256), 1)

    def paired(n):
        return (n % 2) * 128 + n // 2

    def gathered(n):
        at = n % 8
        place = jnp.where(at < 4, 3 - at, at)
        return ((n % 128) // 8) * 16 + place * 2 + n // 128

    perm_a[...] = one_hot(col == paired(row))
    perm_at[...] = one_hot(row == paired(col))
    perm_b[...] = one_hot(col == gathered(row))
    perm_bt[...] = one_hot(row == gathered(col))

    natural = jnp.concatenate([order[...].astype(F32), jnp.zeros((4, HALF), F32)], axis=0)
    high = jnp.floor(natural * 0.5)
    lane_to = iota((HALF, 512), 1)
    stripe = one_hot(
        iota((HALF, 512), 0)
        == (lane_to // 4 % 4) * 32 + (lane_to // 64 % 4) * 8 + (lane_to % 4) * 2 + lane_to // 256
    )
    spread = 2.0 * dot(high.astype(BF), stripe) + dot((natural - 2.0 * high).astype(BF), stripe)
    from_row = iota((8, 512), 0) == iota((8, 512), 1) // 16 % 4
    keys = jnp.sum(jnp.where(from_row, spread, 0.0), axis=0, keepdims=True)
    key_rows = [keys[:, n * HALF : (n + 1) * HALF] for n in range(4)]
    key_cols = jnp.transpose(
        jnp.concatenate(key_rows + [jnp.zeros((HALF - 4, HALF), F32)], axis=0)
    ).astype(I32)

    lax.fori_loop(0, 4, edge_band, 0)
    rims[0].wait()
    rims[1].wait()
    conv(0, (0, 3))
    d_start(0)
    conv(1, (0, 3))
    d_start(1)
    forward_rows()

    loads[1].wait()
    for n in range(4):
        hot = one_hot(iota((HALF, MODES), 1) == key_cols[:, n : n + 1])
        both = jnp.concatenate([dot(hot, wav[r]).astype(BF) for r in range(2)], axis=0)
        tab[n * 256 : (n + 1) * 256, :] = dot(perm_a[...], both).astype(BF)

    def each_device(remote, local):
        def step(i, carry):
            y = wrap(lat_y + i, 4)
            for dz in (4, 3, -3, 2, -2, 1, -1, 0):
                z = wrap(lat_z + dz, 8)
                for dx in (1, 0):
                    x = wrap(lat_x + dx, 2)
                    xz = x * 8 + z
                    for h, g in ((far_h, my_g), (far_h, 1 - my_g), (my_h, 1 - my_g), (my_h, my_g)):
                        peer = (xz * 4 + y, h, g, y * 64 + xz * 4 + 2 * h + g)
                        if dz == 0 and dx == 0 and h is my_h and g is my_g:
                            pl.when(i != 0)(lambda: remote(*peer))
                            pl.when(i == 0)(lambda: local(*peer))
                        else:
                            remote(*peer)
            return carry

        lax.fori_loop(0, 4, step, 0)

    def s_send_blocks(t, first, last):
        target = srecv.at[t * 256 + my_g * 128 + my_src, first:last]
        arrival = s_recv.at[t]

        def remote(to_lat, h, g, pos):
            pltpu.make_async_remote_copy(
                ssend.at[t * 256 + pos, first:last], target, s_send, arrival,
                device_id=(to_lat, 2 * h + g), device_id_type=MESH,
            ).start()

        def local(to_lat, h, g, pos):
            pltpu.make_async_copy(ssend.at[t * 256 + pos, first:last], target, arrival).start()

        each_device(remote, local)

    def wave(t, first, last):
        waved = dot(tab[t * 512 : (t + 1) * 512, :], full[:, first * HALF : last * HALF])
        for c in range(first, last):
            at = (c - first) * HALF
            ssend[t * 256 : (t + 1) * 256, c] = (
                waved[:, at : at + HALF].reshape(256, 2, HALF).astype(BF)
            )

    wait_rows()
    for c in (2, 3):
        conv(c, (0, 1, 2, 3))
        d_start(c)
    d_wait(0)
    wave(0, 0, 1)
    s_send_blocks(0, 0, 1)
    d_wait(1)
    wave(0, 1, 2)
    s_send_blocks(0, 1, 2)

    loads[3].wait()
    for t in range(2):
        least = modes[(lat * LONS + lon) * 2 + t]
        masked = jnp.where(iota((MODES, MODES), 0) >= least, leg[t].astype(F32), 0.0)
        leg[t] = masked.astype(BF)
        leg_t[t] = jnp.transpose(masked).astype(BF)
    loads[6].wait()
    fmat[0:CH, 0:CH] = w_filt[0]
    fmat[0:CH, CH : 2 * CH] = w_filt[1]
    fmat[CH : 2 * CH, 0:CH] = -w_filt[1]
    fmat[CH : 2 * CH, CH : 2 * CH] = w_filt[0]

    d_wait(2)
    d_wait(3)
    wave(0, 2, 4)
    s_send_blocks(0, 2, 4)
    wave(1, 0, 4)
    s_send_blocks(1, 0, 4)

    loads[2].wait()
    for n in range(4):
        hot = one_hot(iota((MODES, HALF), 0) == key_rows[n].astype(I32))
        both = jnp.concatenate([dot(wav_t[r], hot).astype(BF) for r in range(2)], axis=1)
        tab_t[:, n * 256 : (n + 1) * 256] = dot(both, perm_at[...]).astype(BF)

    def b_send_blocks(t, first, last, arrival):
        target = srecv2.at[t * 256 + my_pos, first:last]

        def source(to_lat, h, g):
            return ssend2.at[t * 256 + g * 128 + to_lat * 2 + h, first:last]

        def remote(to_lat, h, g, pos):
            pltpu.make_async_remote_copy(
                source(to_lat, h, g), target, b_send, arrival,
                device_id=(to_lat, 2 * h + g), device_id_type=MESH,
            ).start()

        def local(to_lat, h, g, pos):
            pltpu.make_async_copy(source(to_lat, h, g), target, arrival).start()

        each_device(remote, local)

    cuts = ((0, 1), (1, 2), (2, 4))
    for t in range(2):
        arrived = srecv.at[t * 256 : (t + 1) * 256]
        pltpu.make_async_copy(arrived, arrived, s_recv.at[t]).wait()
        for b in range(4):
            sides = [
                srecv[t * 256 + g * 128 + b * 32 : t * 256 + g * 128 + (b + 1) * 32].reshape(
                    256, HALF
                )
                for g in range(2)
            ]
            turned = dot(perm_b[...], jnp.concatenate(sides, axis=1)).astype(BF)
            for r in range(2):
                spec[b * 128 : (b + 1) * 128, r * CH : (r + 1) * CH] = turned[
                    r * 128 : (r + 1) * 128, :
                ]
        coeffs = dot(leg[t], spec[...]).astype(BF)
        filtered = dot(coeffs, fmat[...]).astype(BF)
        back = dot(leg_t[t], filtered)
        scale = jnp.where(modes[(lat * LONS + lon) * 2 + t] == 0, 1.0, 2.0).astype(F32)
        spec[...] = (back * scale).astype(BF)
        for b in range(4):
            stacked = jnp.concatenate(
                [spec[b * 128 : (b + 1) * 128, r * CH : (r + 1) * CH] for r in range(2)], axis=0
            )
            turned = dot(perm_bt[...], stacked)
            for g in range(2):
                ssend2[t * 256 + g * 128 + b * 32 : t * 256 + g * 128 + (b + 1) * 32] = (
                    turned[:, g * HALF : (g + 1) * HALF].reshape(32, 4, 2, HALF).astype(BF)
                )
        if t == 0:
            b_send_blocks(0, 0, 4, b_recv.at[0])
        else:
            for n, (first, last) in enumerate(cuts):
                b_send_blocks(1, first, last, b_recv.at[1 + n])

    loads[4].wait()
    loads[5].wait()

    def unpack(t, first, last):
        for c in range(first, last):
            zed[t, :, c * HALF : (c + 1) * HALF] = srecv2[t * 256 : (t + 1) * 256, c].reshape(
                512, HALF
            )

    near = my_h * 2 + 1 - my_g

    arrived = srecv2.at[0:256]
    pltpu.make_async_copy(arrived, arrived, b_recv.at[0]).wait()
    unpack(0, 0, 4)

    def first_half(n, carry):
        part = rows_of(n * 256, 256)
        acc[part, :] = dot(tab_t[part, 0:512], zed[0])
        return carry

    lax.fori_loop(0, 4, first_half, 0)

    def second_half(c):
        lanes = slice(c * HALF, (c + 1) * HALF)
        target = precv.at[c * 4 + lon]
        arrival = p_recv.at[c * 2 + my_h]
        for to in (far_h * 2 + my_g, far_h * 2 + 1 - my_g, near, lon):
            part = rows_of(to * COLS, COLS)
            total = acc[part, lanes] + dot(tab_t[part, 512:1024], zed[1, :, lanes])
            psend[c, part, :] = total.astype(BF)
            if to is lon:
                pltpu.make_async_copy(psend.at[c, part, :], target, arrival).start()
            else:
                pltpu.make_async_remote_copy(
                    psend.at[c, part, :], target, p_send, arrival,
                    device_id=(lat, to), device_id_type=MESH,
                ).start()

    def mlp(c):
        def one(n, carry):
            h = jnp.where(n == 0, my_h, far_h)
            first = c * 4 + 2 * h
            arrived = precv.at[pl.ds(first, 2)]
            pltpu.make_async_copy(arrived, arrived, p_recv.at[c * 2 + h]).wait()
            mixed = jnp.concatenate(
                [
                    gelu(precv[first + g].astype(F32) + dsend[first + g].astype(F32))
                    for g in range(2)
                ],
                axis=1,
            ).astype(BF)
            hidden = gelu(dot(mixed, w_in[...])).astype(BF)
            a = row_of(c, h)
            result = ext[a + 2, RIM : RIM + COLS, :].astype(F32) + dot(hidden, w_out[...])
            rows[a] = result.astype(BF)
            pltpu.make_async_copy(rows.at[a], out.at[a], o_sem).start()
            return carry

        lax.fori_loop(0, 2, one, 0)

    for n, (first, last) in enumerate(cuts):
        arrived = srecv2.at[256:512, first:last]
        pltpu.make_async_copy(arrived, arrived, b_recv.at[1 + n]).wait()
        for c in range(first, last):
            unpack(1, c, c + 1)
            second_half(c)
    for c in range(4):
        mlp(c)

    @pl.when((lat == 0) | (lat == 63))
    def _():
        pltpu.make_async_copy(relay, relay, relay_sem.at[1]).wait()

    pltpu.make_async_copy(dsend.at[0:12], dsend.at[0:12], d_send).wait()
    pltpu.make_async_copy(ssend.at[0:510], ssend.at[0:510], s_send).wait()
    pltpu.make_async_copy(ssend2.at[0:510], ssend2.at[0:510], b_send).wait()
    pltpu.make_async_copy(precv.at[0:12], precv.at[0:12], p_send).wait()
    pltpu.make_async_copy(rows, rows, o_sem).wait()


def shards(
    grid_field, basis_index, quad_weight, disco_weight, mode_order, legendre, filter_weight,
    inner_weight, outer_weight,
):
    table = wave_tables()
    waves = jnp.asarray(table, BF)
    waves_t = jnp.asarray(np.swapaxes(table, 1, 2), BF)
    vmem = pl.BlockSpec(memory_space=pltpu.VMEM)
    smem = pl.BlockSpec(memory_space=pltpu.SMEM)
    anywhere = pl.BlockSpec(memory_space=pl.ANY)
    hbm = pl.BlockSpec(memory_space=pltpu.HBM)
    dma = pltpu.SemaphoreType.DMA
    scratch = [
        pltpu.VMEM((ROWS + 4, COLS + 2 * RIM, CH), BF),
        pltpu.VMEM((2, 512, HALF), BF),
        pltpu.VMEM((1024, NLON), BF),
        pltpu.VMEM((NLON, 1024), BF),
        pltpu.VMEM((2, MODES, NLON), BF),
        pltpu.VMEM((2, NLON, MODES), BF),
        pltpu.VMEM((ROWS, 4 * TILE, 512), BF),
        pltpu.VMEM((TILE, 512), I32),
        pltpu.VMEM((20, 8, 512), F32),
        pltpu.VMEM((16, COLS, HALF), BF),
        pltpu.VMEM((NLON, 512), BF),
        pltpu.VMEM((512, 4, 2, HALF), BF),
        pltpu.VMEM((512, 4, 2, HALF), BF),
        pltpu.VMEM((512, 512), BF),
        pltpu.VMEM((2, 512, 512), BF),
        pltpu.VMEM((2, 512, 512), BF),
        pltpu.VMEM((512, 512), BF),
        pltpu.VMEM((512, 4, 2, HALF), BF),
        pltpu.VMEM((512, 4, 2, HALF), BF),
        pltpu.VMEM((2, 512, 512), BF),
        pltpu.VMEM((NLON, 512), F32),
        pltpu.VMEM((4, NLON, HALF), BF),
        pltpu.VMEM((16, COLS, HALF), BF),
        pltpu.VMEM((256, 256), BF),
        pltpu.VMEM((256, 256), BF),
        pltpu.VMEM((256, 256), BF),
        pltpu.VMEM((256, 256), BF),
        pltpu.VMEM((CH, 512), BF),
        pltpu.VMEM((512, CH), BF),
        pltpu.VMEM((2, CH, CH), BF),
        pltpu.VMEM((ROWS, COLS, CH), BF),
        pltpu.VMEM((2, HALF, CH), BF),
        dma((8,)),
        dma((8,)),
        dma((8,)),
        dma((2,)),
        dma,
        dma((4,)),
        dma,
        dma((2,)),
        dma,
        dma((4,)),
        dma,
        dma((8,)),
        dma,
    ]
    return pl.pallas_call(
        layer,
        out_shape=pltpu.VMEM((ROWS, COLS, CH), BF),
        in_specs=[
            hbm, vmem, vmem, hbm, vmem, smem, hbm, hbm, hbm, hbm,
            hbm, hbm,
        ],
        out_specs=anywhere,
        scratch_shapes=scratch,
        compiler_params=pltpu.CompilerParams(
            collective_id=0, has_side_effects=True, vmem_limit_bytes=56 * 1024 * 1024
        ),
        name="layer",
    )(
        grid_field, basis_index, quad_weight, disco_weight, mode_order.reshape(4, HALF), mode_order,
        legendre, filter_weight, inner_weight, outer_weight, waves, waves_t,
    )


def solution(mesh):
    in_specs = (
        P("lat", "lon", None),
        P("lat", None),
        P("lat", None),
        P(),
        P(),
        P(("lat", "lon"), None, None),
        P(),
        P(),
        P(),
    )
    out_specs = P("lat", "lon", None)
    return jax.shard_map(shards, mesh=mesh, in_specs=in_specs, out_specs=out_specs, check_vma=False)
```
